32 devices in a mesh: row: 4 (over y, x), col: 8 (over z, core).
Axes of the slice: x: 2, y: 2, z: 4, core: 2. Of those that a mesh axis runs over, the one named last changes fastest.
Arguments:
- send_blocks: bfloat16 [16, 16, 128, 128], P('row', 'col'), may hold values from -0.125 to 0.125
- send_count: int32 [16, 8], P('row', 'col'), may hold values from 0 to 2, as said below
- send_place: int32 [16, 16], P('row', 'col'), may hold values from 0 to 31, as said below
- term_current: bfloat16 [2, 1024, 8192], P(None, 'row', 'col'), may hold values from -6 to 6
- term_previous: bfloat16 [8192, 8192], P('row', 'col'), may hold values from -6 to 6
- keep_mask: int32 [64, 64], P('row', 'col'), may hold values 0 or 1
Outputs:
- term_next: bfloat16 [8192, 8192], P('row', 'col')
The draws below stay inside these ranges and needn't reach their ends.
Inputs may be any that keep to these rules, and one draw needn't show every extreme that they name: `send_count`: records from sending row s to receiving row d in column c. In every draw some receiver gets 2 from every sending row, and every receiver gets 2 from at least one sending row. `send_place`: over all live records to one receiver (same receiving row and column) the places are distinct. Slots past the count hold 0.
All inputs are finite; a program needn't handle non-finite values. No bound on the sum of `keep_mask` on one device may be relied on, other than what follows from the above.
Results may differ from the reference program's by a relative error of at most 0.001.
Values may be sent and summed in bfloat16 or wider, within the bound.
No kernel may reach another device: no remote copies, remote signals or barrier semaphores. Data moves between devices by JAX's collectives and lax.ppermute only.
A program may use at most 128 MiB of HBM per device.

```python
import jax
import jax.numpy as jnp
from jax import lax

BLOCK = 128
PANELS = 2
CAPACITY = 2
ROW_BLOCKS = 16
GRID_ROWS = 4
GRID_COLS = 8
ROUTE_PAIRS = 16
POSITIONS = 32
PANEL_WIDTH = 1024
ALL_ROW_BLOCKS = 64
ALL_COL_BLOCKS = 64


def route_plan(key):
    streams = jax.random.split(jax.random.fold_in(key, 31), 5)
    counts = jax.random.randint(streams[0], (GRID_ROWS, GRID_ROWS, GRID_COLS), 0, CAPACITY + 1)
    forced = jax.random.randint(streams[1], (1, GRID_ROWS, GRID_COLS), 0, GRID_ROWS)
    sources = jnp.arange(GRID_ROWS, dtype=jnp.int32)[:, None, None]
    counts = jnp.where(sources == forced, CAPACITY, counts)
    full_row = jax.random.randint(streams[2], (), 0, GRID_ROWS)
    full_col = jax.random.randint(streams[3], (), 0, GRID_COLS)
    dest_rows = jnp.arange(GRID_ROWS, dtype=jnp.int32)[None, :, None]
    dest_cols = jnp.arange(GRID_COLS, dtype=jnp.int32)[None, None, :]
    counts = jnp.where((dest_rows == full_row) & (dest_cols == full_col), CAPACITY, counts).astype(jnp.int32)
    scores = jax.random.randint(streams[4], (GRID_ROWS, GRID_COLS, POSITIONS), 0, 1 << 20) * POSITIONS
    scores = scores + jnp.arange(POSITIONS, dtype=jnp.int32)
    ordering = jnp.argsort(scores, axis=-1).astype(jnp.int32)
    offsets = jnp.cumsum(counts, axis=0) - counts
    slot_index = jnp.arange(CAPACITY, dtype=jnp.int32)
    picks = (offsets[..., None] + slot_index).astype(jnp.int32)
    spread = jnp.broadcast_to(ordering[None], (GRID_ROWS, GRID_ROWS, GRID_COLS, POSITIONS))
    places = jnp.take_along_axis(spread, picks, axis=-1)
    places = jnp.where(slot_index < counts[..., None], places, 0).astype(jnp.int32)
    return (counts, places)


def draw_send_count(key, part):
    counts, places = route_plan(key)
    return counts.reshape(ROUTE_PAIRS, GRID_COLS).astype(jnp.int32)


def draw_send_place(key, part):
    counts, places = route_plan(key)
    return places.reshape(ROUTE_PAIRS, GRID_COLS * CAPACITY).astype(jnp.int32)


def place_ends(array, stream_key, low, top_value):
    longest = array.shape.index(max(array.shape))
    spots = []
    for shift in (0, 1):
        where = [jax.random.randint(jax.random.fold_in(stream_key, axis), (), 0, length) for axis, length in enumerate(array.shape)]
        where[longest] = (where[longest] + shift) % array.shape[longest]
        spots.append(tuple(where))
    return array.at[spots[0]].set(low).at[spots[1]].set(top_value)


def block_scale(stream_key, shape, cuts, least, high):
    loudness, own = 1.0, jax.random.fold_in(stream_key, 6)
    for dim, parts in cuts:
        steps = jnp.exp(jax.random.uniform(jax.random.fold_in(own, dim), (parts,), jnp.float32, least / len(cuts), high / len(cuts)))
        loudness = loudness * jnp.repeat(steps, shape[dim] // parts).reshape([-1 if axis == dim else 1 for axis in range(len(shape))])
    return loudness


def scatter_about(own_key, dims, width, bound, cuts=(), held_as=jnp.bfloat16):
    result = jax.random.normal(own_key, dims, jnp.float32) * width
    if len(cuts) > 0:
        result = block_scale(own_key, dims, cuts, -0.22, 0.18) * result
    return jnp.clip(result, min=-bound, max=bound).astype(held_as)


def setup_inputs(seed: int = 0) -> dict:
    keys = jax.random.split(jax.random.key(seed), 7)
    send_blocks = scatter_about(keys[0], (ROUTE_PAIRS, GRID_COLS * CAPACITY, BLOCK, BLOCK), (PANELS * PANEL_WIDTH) ** -0.5, 0.125, ((0, 4), (1, 8)))
    send_count = draw_send_count(jax.random.fold_in(keys[6], 71), 0)
    send_place = draw_send_place(jax.random.fold_in(keys[6], 71), 0)
    term_current = scatter_about(keys[3], (PANELS, PANEL_WIDTH, ALL_COL_BLOCKS * BLOCK), 1.0, 6.0, ((1, 4), (2, 8)))
    term_previous = scatter_about(keys[4], (ALL_ROW_BLOCKS * BLOCK, ALL_COL_BLOCKS * BLOCK), 1.0, 6.0, ((0, 4), (1, 8)))
    keep_mask = place_ends((jax.random.randint(keys[5], (ALL_ROW_BLOCKS, ALL_COL_BLOCKS), 0, 4) < 3).astype(jnp.int32), jax.random.fold_in(keys[5], 1), 0, 1)
    return dict(send_blocks=send_blocks, send_count=send_count, send_place=send_place, term_current=term_current, term_previous=term_previous, keep_mask=keep_mask)


def reference(send_blocks, send_count, send_place, term_current, term_previous, keep_mask):
    pair_index = jnp.arange(ROUTE_PAIRS, dtype=jnp.int32)
    receiver_row = pair_index % GRID_ROWS
    slot_index = (jnp.arange(GRID_COLS * CAPACITY, dtype=jnp.int32) % CAPACITY).astype(jnp.int32)
    column_index = (jnp.arange(GRID_COLS * CAPACITY, dtype=jnp.int32) // CAPACITY).astype(jnp.int32)
    count_wide = jnp.repeat(send_count, CAPACITY, axis=1).astype(jnp.int32)
    is_live = slot_index[None, :] < count_wide
    block_row = receiver_row[:, None] * ROW_BLOCKS + send_place // PANELS
    panel_index = send_place % PANELS
    target = (block_row * PANELS + panel_index) * GRID_COLS + column_index[None, :]
    outside = ALL_ROW_BLOCKS * PANELS * GRID_COLS
    target = jnp.where(is_live, target, outside).astype(jnp.int32)
    blank_tile = jnp.zeros((outside, BLOCK, BLOCK), jnp.bfloat16)
    placed = blank_tile.at[target.reshape(-1)].set(send_blocks.reshape(-1, BLOCK, BLOCK), mode="drop")
    hamiltonian = placed.reshape(ALL_ROW_BLOCKS, PANELS * GRID_COLS, BLOCK, BLOCK)
    term_flat = term_current.reshape(PANELS * PANEL_WIDTH, ALL_COL_BLOCKS * BLOCK)
    previous = term_previous.reshape(ALL_ROW_BLOCKS, BLOCK, ALL_COL_BLOCKS * BLOCK)

    def one_row(operands):
        row_blocks, row_keep, row_previous = operands
        row_matrix = jnp.transpose(row_blocks, (1, 0, 2)).reshape(BLOCK, PANELS * PANEL_WIDTH)
        product = jnp.dot(row_matrix, term_flat, preferred_element_type=jnp.float32)
        wanted = jnp.repeat(row_keep, BLOCK) > 0
        update = 2.0 * product - row_previous.astype(jnp.float32)
        return jnp.where(wanted[None, :], update, jnp.zeros_like(update)).astype(jnp.bfloat16)

    rows_out = lax.map(one_row, (hamiltonian, keep_mask, previous))
    return rows_out.reshape(ALL_ROW_BLOCKS * BLOCK, ALL_COL_BLOCKS * BLOCK)
```

```python
import functools

import jax
import jax.numpy as jnp
from jax import lax
from jax.experimental import pallas as pl
from jax.experimental.pallas import tpu as pltpu
from jax.sharding import PartitionSpec as P

PAD = 16
TILE = 256


def swap(x, axis, offset):
    size = lax.axis_size(axis)
    return lax.ppermute(x, axis, [(i, i ^ offset) for i in range(size)])


def early_kernel(
    dims, codes, spot, *refs
):
    grid_rows, grid_cols, slots, panels, block = dims
    span = slots * block + PAD
    per_row = grid_cols // grid_rows
    own_refs = refs[:grid_cols]
    rest_refs = refs[grid_cols : 2 * grid_cols]
    term_refs = refs[2 * grid_cols : -7]
    previous, acc, late, matrix, terms, held, sems = refs[-7:]
    depth = per_row * block
    early = matrix.shape[0]

    @pl.when(pl.program_id(0) == 0)
    def _():
        copies = []
        for o in range(grid_cols):
            copies.append(pltpu.make_async_copy(own_refs[o], held.at[o, pl.ds(0, span)], sems.at[0]))
            copies.append(
                pltpu.make_async_copy(
                    rest_refs[o], held.at[o, pl.ds(span, (grid_rows - 1) * span)], sems.at[0]
                )
            )
        at = 0
        for ref in term_refs:
            rows = ref.shape[0]
            copies.append(pltpu.make_async_copy(ref, terms.at[pl.ds(at, rows)], sems.at[0]))
            at += rows
        for copy in copies:
            copy.start()
        matrix[...] = jnp.zeros_like(matrix)
        late[...] = jnp.zeros_like(late)
        for copy in copies:
            copy.wait()
        my_row, my_col = spot[0], spot[1]

        def place(n, carry):
            o = n // grid_rows
            s = n % grid_rows
            col = my_col ^ o
            source = (col // per_row) ^ my_row
            inner = col % per_row
            for j in range(slots):
                code = codes[n * slots + j]
                row = code // panels
                k = (source * panels + code % panels) * per_row + inner
                at = pl.multiple_of(row * block, block)
                first = pl.multiple_of(s * span + j * block, PAD)

                @pl.when((code >= 0) & (k < early))
                def _():
                    matrix[k, pl.ds(at, block), :] = held[o, pl.ds(first, block), :]

                @pl.when((code >= 0) & (k >= early))
                def _():
                    late[k - early, pl.ds(at, block), :] = held[o, pl.ds(first, block), :]

            return carry

        lax.fori_loop(0, grid_cols * grid_rows, place, 0)

    base = pl.multiple_of(pl.program_id(0) * TILE, TILE)
    left = jnp.concatenate([matrix[k, pl.ds(base, TILE), :] for k in range(early)], axis=1)
    product = jnp.dot(left, terms[...], preferred_element_type=jnp.float32)
    acc[...] = 2.0 * product - previous[...].astype(jnp.float32)


def late_kernel(dims, keep, acc, late, *refs):
    block = dims[-1]
    term_refs, out = refs[:-1], refs[-1]
    blocks = late.shape[0]
    left = jnp.concatenate([late[k] for k in range(blocks)], axis=1)
    right = jnp.concatenate([ref[...] for ref in term_refs], axis=0)
    product = jnp.dot(left, right, preferred_element_type=jnp.float32)
    update = acc[...] + 2.0 * product
    per_tile = TILE // block
    step = pl.program_id(0)
    for i in range(per_tile):
        for j in range(out.shape[1] // block):
            wanted = keep[step * per_tile + i, j] > 0
            part = update[i * block : (i + 1) * block, j * block : (j + 1) * block]
            out[pl.ds(i * block, block), pl.ds(j * block, block)] = jnp.where(
                wanted, part, jnp.zeros_like(part)
            ).astype(out.dtype)


def per_device(send_blocks, send_count, send_place, term_current, term_previous, keep_mask):
    grid_rows, grid_cols = lax.axis_size("row"), lax.axis_size("col")
    my_row, my_col = lax.axis_index("row"), lax.axis_index("col")
    block = send_blocks.shape[-1]
    slots = send_blocks.shape[1]
    panels = term_current.shape[0]
    tile_rows, tile_cols = term_previous.shape
    per_row = grid_cols // grid_rows
    dims = (grid_rows, grid_cols, slots, panels, block)

    lane = jnp.arange(slots, dtype=jnp.int32)
    places = jnp.where(lane[None, :] < send_count, send_place, -1).astype(jnp.bfloat16)
    pad = jnp.broadcast_to(
        jnp.pad(places, ((0, 0), (0, block - slots)))[:, None, :], (grid_rows, PAD, block)
    )

    def payload(offset):
        to = my_row ^ offset
        records = lax.dynamic_index_in_dim(send_blocks, to, 0, keepdims=False)
        tail = lax.dynamic_index_in_dim(pad, to, 0, keepdims=False)
        return jnp.concatenate([records.reshape(slots * block, block), tail], axis=0)

    own = payload(0)
    got = [swap(payload(o), "row", o) for o in range(1, grid_rows)]

    mine = [term_current[p] for p in range(panels)]
    term = {}
    last = grid_rows - 1
    if grid_rows == 4 and panels == 2:
        term[1, 0] = swap(mine[0], "row", 1)
        term[2, 1] = swap(mine[1], "row", 2)
        term[1, 1] = swap(mine[1], "row", 1)
        term[2, 0] = swap(mine[0], "row", 2)
        term[3, 0] = swap(term[1, 0], "row", 2)
        term[3, 1] = swap(term[2, 1], "row", 1)
    else:
        for o in range(1, grid_rows):
            for p in range(panels):
                term[o, p] = swap(mine[p], "row", o)

    rest = jnp.concatenate(got, axis=0)
    owns, rests = {0: own}, {0: rest}
    for o in range(2, grid_cols, 2):
        owns[o] = swap(own, "col", o)
        rests[o] = swap(rest, "col", o)
    for o in range(0, grid_cols, 2):
        owns[o ^ 1] = swap(owns[o], "col", 1)
        rests[o ^ 1] = swap(rests[o], "col", 1)
    span = slots * block + PAD
    codes = []
    for o in range(grid_cols):
        codes.append(owns[o][slots * block, :slots])
        for s in range(grid_rows - 1):
            codes.append(rests[o][s * span + slots * block, :slots])
    codes = jnp.concatenate(codes).astype(jnp.int32)

    early = (grid_rows - 1) * panels * per_row
    any_spec = pl.BlockSpec(memory_space=pl.ANY)
    smem_spec = pl.BlockSpec(memory_space=pltpu.SMEM)
    early_terms = [term_current.reshape(-1, tile_cols)] + [
        term[o, p] for o in range(1, last) for p in range(panels)
    ]
    late_blocks = panels * per_row
    steps = tile_rows // TILE
    acc, late = pl.pallas_call(
        functools.partial(early_kernel, dims),
        grid=(steps,),
        out_shape=[
            jax.ShapeDtypeStruct((tile_rows, tile_cols), jnp.float32),
            jax.ShapeDtypeStruct((late_blocks, tile_rows, block), jnp.bfloat16),
        ],
        in_specs=[smem_spec, smem_spec]
        + [any_spec] * (2 * grid_cols + len(early_terms))
        + [pl.BlockSpec((TILE, tile_cols), lambda i: (i, 0))],
        out_specs=[
            pl.BlockSpec((TILE, tile_cols), lambda i: (i, 0)),
            pl.BlockSpec((late_blocks, tile_rows, block), lambda i: (0, 0, 0)),
        ],
        scratch_shapes=[
            pltpu.VMEM((early, tile_rows, block), jnp.bfloat16),
            pltpu.VMEM((early * block, tile_cols), jnp.bfloat16),
            pltpu.VMEM((grid_cols, grid_rows * span, block), jnp.bfloat16),
            pltpu.SemaphoreType.DMA((1,)),
        ],
        compiler_params=pltpu.CompilerParams(vmem_limit_bytes=48 * 1024 * 1024),
        cost_estimate=pl.CostEstimate(
            flops=2 * tile_rows * tile_cols * early * block,
            bytes_accessed=tile_rows * tile_cols * 6,
            transcendentals=0,
        ),
        name="early_product",
    )(
        codes,
        jnp.stack([my_row, my_col]).astype(jnp.int32),
        *[owns[o] for o in range(grid_cols)],
        *[rests[o] for o in range(grid_cols)],
        *early_terms,
        term_previous,
    )
    return pl.pallas_call(
        functools.partial(late_kernel, dims),
        grid=(steps,),
        out_shape=jax.ShapeDtypeStruct((tile_rows, tile_cols), term_previous.dtype),
        in_specs=[
            smem_spec,
            pl.BlockSpec((TILE, tile_cols), lambda i: (i, 0)),
            pl.BlockSpec((late_blocks, TILE, block), lambda i: (0, i, 0)),
        ]
        + [pl.BlockSpec(term[last, p].shape, lambda i: (0, 0)) for p in range(panels)],
        out_specs=pl.BlockSpec((TILE, tile_cols), lambda i: (i, 0)),
        compiler_params=pltpu.CompilerParams(vmem_limit_bytes=32 * 1024 * 1024),
        cost_estimate=pl.CostEstimate(
            flops=2 * tile_rows * tile_cols * late_blocks * block,
            bytes_accessed=tile_rows * tile_cols * 6,
            transcendentals=0,
        ),
        name="late_product",
    )(keep_mask, acc, late, *[term[last, p] for p in range(panels)])


def solution(mesh):
    placed = (
        P("row", "col", None, None),
        P("row", "col"),
        P("row", "col"),
        P(None, "row", "col"),
        P("row", "col"),
        P("row", "col"),
    )
    return jax.shard_map(
        per_device, mesh=mesh, in_specs=placed, out_specs=P("row", "col"), check_vma=False
    )
```

```python
import functools

import jax
import jax.numpy as jnp
from jax import lax
from jax.experimental import pallas as pl
from jax.experimental.pallas import tpu as pltpu
from jax.sharding import PartitionSpec as P

SLACK = 5 * 1024 * 1024
SMALL = 1024 * 1024
PAD = 16
TILE = 256


def swap(x, axis, offset):
    size = lax.axis_size(axis)
    return lax.ppermute(x, axis, [(i, i ^ offset) for i in range(size)])


def mark_kernel(*refs):
    refs[-1][...] = jnp.zeros_like(refs[-1])


def mark(arrays):
    return pl.pallas_call(
        mark_kernel,
        out_shape=jax.ShapeDtypeStruct((PAD, 128), jnp.bfloat16),
        in_specs=[pl.BlockSpec(memory_space=pl.ANY)] * len(arrays),
        compiler_params=pltpu.CompilerParams(vmem_limit_bytes=SMALL),
        name="mark",
    )(*arrays)


def hold_kernel(*refs):
    pass


def hold(array, others):
    return pl.pallas_call(
        hold_kernel,
        out_shape=jax.ShapeDtypeStruct(array.shape, array.dtype),
        in_specs=[pl.BlockSpec(memory_space=pl.ANY)] * (1 + len(others)),
        out_specs=pl.BlockSpec(memory_space=pl.ANY),
        input_output_aliases={0: 0},
        compiler_params=pltpu.CompilerParams(vmem_limit_bytes=SMALL),
        name="hold",
    )(array, *others)


def early_kernel(dims, arrays, early, spot, offsets, *refs):
    grid_rows, grid_cols, slots, panels, block = dims
    span = slots * block + PAD
    per_row = grid_cols // grid_rows
    record_refs = refs[:arrays]
    term_refs = refs[arrays:-12]
    previous, acc, late, terms, held, before, code_rows, codes, counts, firsts, depths, sems = refs[-12:]
    row_blocks = acc.shape[0] // block
    count = grid_rows * grid_cols
    nothing = count * span

    def fetch(sources, target, sem):
        copies, at = [], 0
        for ref in sources:
            rows = ref.shape[0]
            copies.append(pltpu.make_async_copy(ref, target.at[pl.ds(at, rows)], sem))
            at += rows
        for copy in copies:
            copy.start()
        return copies

    first = fetch(record_refs, held, sems.at[0])
    second = fetch(term_refs, terms, sems.at[1])
    third = fetch([previous], before, sems.at[2])
    late[...] = jnp.zeros_like(late)
    held[pl.ds(nothing, block), :] = jnp.zeros((block, held.shape[1]), held.dtype)

    def clear(i, carry):
        counts[i] = 0
        for n in range(early):
            firsts[i, n] = nothing
            depths[i, n] = 0
        return carry

    lax.fori_loop(0, row_blocks, clear, 0)
    for copy in first:
        copy.wait()
    for n in range(count):
        row = held[pl.ds(n * span + slots * block, PAD), :].astype(jnp.float32)
        code_rows[pl.ds(n, 1), :] = row[:1].astype(jnp.int32)
    to_scalars = pltpu.make_async_copy(code_rows, codes, sems.at[3])
    to_scalars.start()
    to_scalars.wait()
    my_row, my_col = spot[0], spot[1]

    def place(n, carry):
        col = my_col ^ offsets[n // grid_rows]
        source = (col // per_row) ^ my_row
        inner = col % per_row
        for j in range(slots):
            code = codes[n, j]
            row = code // panels
            k = (source * panels + code % panels) * per_row + inner
            start = pl.multiple_of(n * span + j * block, PAD)

            @pl.when((code >= 0) & (k < early))
            def _():
                at = counts[row]
                firsts[row, at] = start
                depths[row, at] = k * block
                counts[row] = at + 1

            @pl.when((code >= 0) & (k >= early))
            def _():
                to = pl.ds(pl.multiple_of(row * block, block), block)
                late[k - early, to, :] = held[pl.ds(start, block), :]

        return carry

    lax.fori_loop(0, count, place, 0)
    for copy in second + third:
        copy.wait()

    def pair(i, n):
        def one(m):
            left = held[pl.ds(pl.multiple_of(firsts[i, m], PAD), block), :]
            right = terms[pl.ds(pl.multiple_of(depths[i, m], block), block), :]
            return left, right

        (left0, right0), (left1, right1) = one(2 * n), one(2 * n + 1)
        return jnp.dot(
            jnp.concatenate([left0, left1], axis=1),
            jnp.concatenate([right0, right1], axis=0),
            preferred_element_type=jnp.float32,
        )

    for i in range(row_blocks):
        rows = pl.ds(i * block, block)
        product = pair(i, 0) + pair(i, 1)
        acc[rows, :] = 2.0 * product - before[rows, :].astype(jnp.float32)

    def more(i, carry):
        rows = pl.ds(pl.multiple_of(i * block, block), block)

        def step(n, inner):
            acc[rows, :] += 2.0 * pair(i, n)
            return inner

        return lax.fori_loop(2, (counts[i] + 1) // 2, step, carry)

    lax.fori_loop(0, row_blocks, more, 0)


def late_kernel(dims, keep, acc, late, *refs):
    block = dims[-1]
    term_refs, out, staged, sem = refs[:-3], refs[-3], refs[-2], refs[-1]
    blocks = late.shape[0]
    right = jnp.concatenate([ref[...] for ref in term_refs], axis=0)
    copies = []
    for t in range(acc.shape[0] // TILE):
        rows = pl.ds(t * TILE, TILE)
        left = jnp.concatenate([late[k, rows, :] for k in range(blocks)], axis=1)
        product = jnp.dot(left, right, preferred_element_type=jnp.float32)
        update = acc[rows, :] + 2.0 * product
        for i in range(TILE // block):
            for j in range(out.shape[1] // block):
                wanted = keep[t * (TILE // block) + i, j] > 0
                part = update[i * block : (i + 1) * block, j * block : (j + 1) * block]
                staged[pl.ds(t * TILE + i * block, block), pl.ds(j * block, block)] = jnp.where(
                    wanted, part, jnp.zeros_like(part)
                ).astype(out.dtype)
        copies.append(pltpu.make_async_copy(staged.at[rows], out.at[rows], sem))
        copies[-1].start()
    for copy in copies:
        copy.wait()


def per_device(send_blocks, send_count, send_place, term_current, term_previous, keep_mask):
    grid_rows, grid_cols = lax.axis_size("row"), lax.axis_size("col")
    my_row, my_col = lax.axis_index("row"), lax.axis_index("col")
    block = send_blocks.shape[-1]
    slots = send_blocks.shape[1]
    panels = term_current.shape[0]
    tile_rows, tile_cols = term_previous.shape
    row_blocks = tile_rows // block
    per_row = grid_cols // grid_rows
    dims = (grid_rows, grid_cols, slots, panels, block)

    lane = jnp.arange(slots, dtype=jnp.int32)
    places = jnp.where(lane[None, :] < send_count, send_place, -1).astype(jnp.bfloat16)
    pad = jnp.broadcast_to(
        jnp.pad(places, ((0, 0), (0, block - slots)))[:, None, :], (grid_rows, PAD, block)
    )

    def payload(offset):
        to = my_row ^ offset
        records = lax.dynamic_index_in_dim(send_blocks, to, 0, keepdims=False)
        tail = lax.dynamic_index_in_dim(pad, to, 0, keepdims=False)
        return jnp.concatenate([records.reshape(slots * block, block), tail], axis=0)

    mine = [term_current[p] for p in range(panels)]
    term = {}
    last = grid_rows - 1
    if grid_rows == 4 and panels == 2:
        term[1, 0] = swap(mine[0], "row", 1)
        term[2, 1] = swap(mine[1], "row", 2)
        term[1, 1] = swap(mine[1], "row", 1)
        term[2, 0] = swap(mine[0], "row", 2)
        term[3, 0] = swap(term[1, 0], "row", 2)
        term[3, 1] = swap(term[2, 1], "row", 1)
    else:
        for o in range(1, grid_rows):
            for p in range(panels):
                term[o, p] = swap(mine[p], "row", o)

    own = jnp.concatenate(
        [payload(0)] + [swap(payload(o), "row", o) for o in range(1, grid_rows)], axis=0
    )
    if grid_cols == 8:
        far, near = swap(own, "col", 6), swap(own, "col", 2)
        if grid_rows == 4:
            far = hold(far, [swap(mark([term[1, 0], term[2, 1]]), "col", 1)])
        middle = swap(far, "col", 2)
        if grid_rows == 4:
            token = swap(mark([term[1, 1], term[2, 0]]), "col", 1)
            middle = hold(middle, [swap(token, "col", 1)])
        offsets = [0, 2, 6, 4]
        parts = [own, near, far, middle]
        groups = [jnp.concatenate(parts[:3], axis=0), middle]
        others = [swap(group, "col", 1) for group in groups]
    else:
        offsets = list(range(0, grid_cols, 2))
        parts = [own] + [swap(own, "col", o) for o in offsets[1:]]
        others = [swap(part, "col", 1) for part in parts]
    offsets = offsets + [o ^ 1 for o in offsets]
    record_arrays = parts + others
    span = slots * block + PAD

    early = (grid_rows - 1) * panels * per_row
    anywhere = pl.BlockSpec(memory_space=pl.ANY)
    smem = pl.BlockSpec(memory_space=pltpu.SMEM)
    vmem = pl.BlockSpec(memory_space=pltpu.VMEM)
    early_terms = [term_current.reshape(-1, tile_cols)] + [
        term[o, p] for o in range(1, last) for p in range(panels)
    ]
    late_blocks = panels * per_row
    count = grid_cols * grid_rows
    early_bytes = 2 * (early * block * tile_cols + count * span * block + tile_rows * tile_cols)
    passed_bytes = 4 * tile_rows * tile_cols + 2 * late_blocks * tile_rows * block
    acc, late = pl.pallas_call(
        functools.partial(early_kernel, dims, len(record_arrays), early),
        out_shape=[
            jax.ShapeDtypeStruct((tile_rows, tile_cols), jnp.float32),
            jax.ShapeDtypeStruct((late_blocks, tile_rows, block), jnp.bfloat16),
        ],
        in_specs=[smem, smem] + [anywhere] * (len(record_arrays) + len(early_terms) + 1),
        out_specs=[vmem, vmem],
        scratch_shapes=[
            pltpu.VMEM((early * block, tile_cols), jnp.bfloat16),
            pltpu.VMEM((count * span + block, block), jnp.bfloat16),
            pltpu.VMEM((tile_rows, tile_cols), jnp.bfloat16),
            pltpu.VMEM((count, block), jnp.int32),
            pltpu.SMEM((count, block), jnp.int32),
            pltpu.SMEM((row_blocks,), jnp.int32),
            pltpu.SMEM((row_blocks, early), jnp.int32),
            pltpu.SMEM((row_blocks, early), jnp.int32),
            pltpu.SemaphoreType.DMA((4,)),
        ],
        compiler_params=pltpu.CompilerParams(vmem_limit_bytes=early_bytes + passed_bytes + SLACK),
        name="early_product",
    )(
        jnp.stack([my_row, my_col]).astype(jnp.int32),
        jnp.array(offsets, jnp.int32),
        *record_arrays,
        *early_terms,
        term_previous,
    )
    return pl.pallas_call(
        functools.partial(late_kernel, dims),
        out_shape=jax.ShapeDtypeStruct((tile_rows, tile_cols), term_previous.dtype),
        in_specs=[smem, vmem, vmem] + [vmem] * panels,
        out_specs=anywhere,
        scratch_shapes=[
            pltpu.VMEM((tile_rows, tile_cols), term_previous.dtype),
            pltpu.SemaphoreType.DMA,
        ],
        compiler_params=pltpu.CompilerParams(vmem_limit_bytes=passed_bytes + 2 * tile_rows * tile_cols + SLACK),
        name="late_product",
    )(keep_mask, acc, late, *[term[last, p] for p in range(panels)])


def solution(mesh):
    placed = (
        P("row", "col", None, None),
        P("row", "col"),
        P("row", "col"),
        P(None, "row", "col"),
        P("row", "col"),
        P("row", "col"),
    )
    return jax.shard_map(
        per_device, mesh=mesh, in_specs=placed, out_specs=P("row", "col"), check_vma=False
    )
```

```python
import functools

import jax
import jax.numpy as jnp
from jax import lax
from jax.experimental import pallas as pl
from jax.experimental.pallas import tpu as pltpu
from jax.sharding import PartitionSpec as P

SLACK = 5 * 1024 * 1024
PAD = 16
TILE = 256


def swap(x, axis, offset):
    size = lax.axis_size(axis)
    return lax.ppermute(x, axis, [(i, i ^ offset) for i in range(size)])


def early_kernel(dims, arrays, early, routes, spot, offsets, *refs):
    grid_rows, grid_cols, slots, panels, block = dims
    span = slots * block + PAD
    per_row = grid_cols // grid_rows
    record_refs = refs[:arrays]
    term_refs = refs[arrays:-11]
    previous, acc, late, terms, held, code_rows, codes, counts, firsts, depths, sems = refs[-11:]
    row_blocks = acc.shape[0] // block
    count = grid_rows * grid_cols
    nothing = count * span

    def fetch(copies):
        for copy in copies:
            copy.start()
        return copies

    at, first = 0, []
    for ref in record_refs:
        rows = pl.ds(at, ref.shape[0])
        first.append(pltpu.make_async_copy(ref, held.at[rows], sems.at[0]))
        at += ref.shape[0]
    first = fetch(first)
    second = []
    for ref, route in zip(term_refs, routes):
        for source, target, size in route:
            here, there = pl.ds(source, size), pl.ds(target, size)
            second.append(pltpu.make_async_copy(ref.at[here], terms.at[there], sems.at[1]))
    second = fetch(second)
    late[...] = jnp.zeros_like(late)
    held[pl.ds(nothing, block), :] = jnp.zeros((block, held.shape[1]), held.dtype)

    def clear(i, carry):
        counts[i] = 0
        for n in range(early):
            firsts[i, n] = nothing
            depths[i, n] = 0
        return carry

    lax.fori_loop(0, row_blocks, clear, 0)
    for copy in first:
        copy.wait()
    for n in range(count):
        row = held[pl.ds(n * span + slots * block, PAD), :].astype(jnp.float32)
        code_rows[pl.ds(n, 1), :] = row[:1].astype(jnp.int32)
    to_scalars = pltpu.make_async_copy(code_rows, codes, sems.at[2])
    to_scalars.start()
    to_scalars.wait()
    my_row, my_col = spot[0], spot[1]

    def place(n, carry):
        col = my_col ^ offsets[n // grid_rows]
        source = (col // per_row) ^ my_row
        inner = col % per_row
        for j in range(slots):
            code = codes[n, j]
            row = code // panels
            k = (source * panels + code % panels) * per_row + inner
            record = pl.multiple_of(n * span + j * block, PAD)

            @pl.when((code >= 0) & (k < early))
            def _():
                at = counts[row]
                firsts[row, at] = record
                depths[row, at] = k * block
                counts[row] = at + 1

            @pl.when((code >= 0) & (k >= early))
            def _():
                to = pl.ds(pl.multiple_of(row * block, block), block)
                late[k - early, to, :] = held[pl.ds(record, block), :]

        return carry

    lax.fori_loop(0, count, place, 0)
    for copy in second:
        copy.wait()

    def pair(i, n):
        def one(m):
            left = held[pl.ds(pl.multiple_of(firsts[i, m], PAD), block), :]
            right = terms[pl.ds(pl.multiple_of(depths[i, m], block), block), :]
            return left, right

        (left0, right0), (left1, right1) = one(2 * n), one(2 * n + 1)
        return jnp.dot(
            jnp.concatenate([left0, left1], axis=1),
            jnp.concatenate([right0, right1], axis=0),
            preferred_element_type=jnp.float32,
        )

    for i in range(row_blocks):
        rows = pl.ds(i * block, block)
        product = pair(i, 0) + pair(i, 1)
        acc[rows, :] = 2.0 * product - previous[rows, :].astype(jnp.float32)

    def more(i, carry):
        rows = pl.ds(pl.multiple_of(i * block, block), block)

        def step(n, inner):
            acc[rows, :] += 2.0 * pair(i, n)
            return inner

        return lax.fori_loop(2, (counts[i] + 1) // 2, step, carry)

    lax.fori_loop(0, row_blocks, more, 0)


def late_kernel(dims, keep, acc, late, *refs):
    block = dims[-1]
    term_refs, out, staged, sem = refs[:-3], refs[-3], refs[-2], refs[-1]
    blocks = late.shape[0]
    right = jnp.concatenate([ref[...] for ref in term_refs], axis=0)
    copies = []
    for t in range(acc.shape[0] // TILE):
        rows = pl.ds(t * TILE, TILE)
        left = jnp.concatenate([late[k, rows, :] for k in range(blocks)], axis=1)
        product = jnp.dot(left, right, preferred_element_type=jnp.float32)
        update = acc[rows, :] + 2.0 * product
        for i in range(TILE // block):
            for j in range(out.shape[1] // block):
                wanted = keep[t * (TILE // block) + i, j] > 0
                part = update[i * block : (i + 1) * block, j * block : (j + 1) * block]
                staged[pl.ds(t * TILE + i * block, block), pl.ds(j * block, block)] = jnp.where(
                    wanted, part, jnp.zeros_like(part)
                ).astype(out.dtype)
        copies.append(pltpu.make_async_copy(staged.at[rows], out.at[rows], sem))
        copies[-1].start()
    for copy in copies:
        copy.wait()


def per_device(send_blocks, send_count, send_place, term_current, term_previous, keep_mask):
    grid_rows, grid_cols = lax.axis_size("row"), lax.axis_size("col")
    my_row, my_col = lax.axis_index("row"), lax.axis_index("col")
    block = send_blocks.shape[-1]
    slots = send_blocks.shape[1]
    panels = term_current.shape[0]
    tile_rows, tile_cols = term_previous.shape
    row_blocks = tile_rows // block
    per_row = grid_cols // grid_rows
    dims = (grid_rows, grid_cols, slots, panels, block)

    lane = jnp.arange(slots, dtype=jnp.int32)
    places = jnp.where(lane[None, :] < send_count, send_place, -1).astype(jnp.bfloat16)
    pad = jnp.broadcast_to(
        jnp.pad(places, ((0, 0), (0, block - slots)))[:, None, :], (grid_rows, PAD, block)
    )

    def payload(offset):
        to = my_row ^ offset
        records = lax.dynamic_index_in_dim(send_blocks, to, 0, keepdims=False)
        tail = lax.dynamic_index_in_dim(pad, to, 0, keepdims=False)
        return jnp.concatenate([records.reshape(slots * block, block), tail], axis=0)

    last = grid_rows - 1
    rows = term_current.shape[1]
    flat = term_current.reshape(panels * rows, tile_cols)
    pieces = [(flat, [(0, 0, panels * rows)])]
    if grid_rows == 4 and panels == 2:
        size = panels * rows
        up, down = swap(flat, "row", 1), swap(flat, "row", 2)
        pieces += [(up, [(0, size, size)]), (down, [(0, 2 * size, size)])]
        final = [swap(up[:rows], "row", 2), swap(down[rows:], "row", 1)]
    else:
        for o in range(1, last):
            pieces.append((swap(flat, "row", o), [(0, o * panels * rows, panels * rows)]))
        final = [swap(flat[p * rows : (p + 1) * rows], "row", last) for p in range(panels)]

    own = jnp.concatenate(
        [payload(0)] + [swap(payload(o), "row", o) for o in range(1, grid_rows)], axis=0
    )
    if grid_cols == 8:
        far, near = swap(own, "col", 6), swap(own, "col", 2)
        middle = swap(far, "col", 2)
        offsets = [0, 2, 6, 4]
        parts = [own, near, far, middle]
        groups = [jnp.concatenate(parts[:3], axis=0), middle]
        parts = groups
        others = [swap(group, "col", 1) for group in groups]
    else:
        offsets = list(range(0, grid_cols, 2))
        parts = [own] + [swap(own, "col", o) for o in offsets[1:]]
        others = [swap(part, "col", 1) for part in parts]
    offsets = offsets + [o ^ 1 for o in offsets]
    record_arrays = parts + others
    span = slots * block + PAD

    early = (grid_rows - 1) * panels * per_row
    anywhere = pl.BlockSpec(memory_space=pl.ANY)
    smem = pl.BlockSpec(memory_space=pltpu.SMEM)
    vmem = pl.BlockSpec(memory_space=pltpu.VMEM)
    late_blocks = panels * per_row
    count = grid_cols * grid_rows
    early_bytes = 2 * (early * block * tile_cols + count * span * block + tile_rows * tile_cols)
    passed_bytes = 4 * tile_rows * tile_cols + 2 * late_blocks * tile_rows * block
    acc, late = pl.pallas_call(
        functools.partial(early_kernel, dims, len(record_arrays), early, [p[1] for p in pieces]),
        out_shape=[
            jax.ShapeDtypeStruct((tile_rows, tile_cols), jnp.float32),
            jax.ShapeDtypeStruct((late_blocks, tile_rows, block), jnp.bfloat16),
        ],
        in_specs=[smem, smem] + [anywhere] * (len(record_arrays) + len(pieces)) + [vmem],
        out_specs=[vmem, vmem],
        scratch_shapes=[
            pltpu.VMEM((early * block, tile_cols), jnp.bfloat16),
            pltpu.VMEM((count * span + block, block), jnp.bfloat16),
            pltpu.VMEM((count, block), jnp.int32),
            pltpu.SMEM((count, block), jnp.int32),
            pltpu.SMEM((row_blocks,), jnp.int32),
            pltpu.SMEM((row_blocks, early), jnp.int32),
            pltpu.SMEM((row_blocks, early), jnp.int32),
            pltpu.SemaphoreType.DMA((3,)),
        ],
        compiler_params=pltpu.CompilerParams(vmem_limit_bytes=early_bytes + passed_bytes + SLACK),
        name="early_product",
    )(
        jnp.stack([my_row, my_col]).astype(jnp.int32),
        jnp.array(offsets, jnp.int32),
        *record_arrays,
        *[p[0] for p in pieces],
        term_previous,
    )
    return pl.pallas_call(
        functools.partial(late_kernel, dims),
        out_shape=jax.ShapeDtypeStruct((tile_rows, tile_cols), term_previous.dtype),
        in_specs=[smem, vmem, vmem] + [vmem] * len(final),
        out_specs=anywhere,
        scratch_shapes=[
            pltpu.VMEM((tile_rows, tile_cols), term_previous.dtype),
            pltpu.SemaphoreType.DMA,
        ],
        compiler_params=pltpu.CompilerParams(vmem_limit_bytes=passed_bytes + 2 * tile_rows * tile_cols + SLACK),
        name="late_product",
    )(keep_mask, acc, late, *final)


def solution(mesh):
    placed = (
        P("row", "col", None, None),
        P("row", "col"),
        P("row", "col"),
        P(None, "row", "col"),
        P("row", "col"),
        P("row", "col"),
    )
    return jax.shard_map(
        per_device, mesh=mesh, in_specs=placed, out_specs=P("row", "col"), check_vma=False
    )
```

```python
import functools

import jax
import jax.numpy as jnp
from jax import lax
from jax.experimental import pallas as pl
from jax.experimental.pallas import tpu as pltpu
from jax.sharding import PartitionSpec as P

SLACK = 5 * 1024 * 1024
PAD = 16
TILE = 256


def swap(x, axis, offset):
    size = lax.axis_size(axis)
    return lax.ppermute(x, axis, [(i, i ^ offset) for i in range(size)])


def early_kernel(dims, arrays, early, routes, spot, offsets, *refs):
    grid_rows, grid_cols, slots, panels, block = dims
    span = slots * block + PAD
    per_row = grid_cols // grid_rows
    record_refs = refs[:arrays]
    term_refs = refs[arrays:-10]
    acc, late, terms, held, code_rows, codes, counts, firsts, depths, sems = refs[-10:]
    row_blocks = acc.shape[0] // block
    count = grid_rows * grid_cols
    nothing = count * span

    def fetch(copies):
        for copy in copies:
            copy.start()
        return copies

    at, first = 0, []
    for ref in record_refs:
        rows = pl.ds(at, ref.shape[0])
        first.append(pltpu.make_async_copy(ref, held.at[rows], sems.at[0]))
        at += ref.shape[0]
    first = fetch(first)
    second = []
    for ref, route in zip(term_refs, routes):
        for source, target, size in route:
            here, there = pl.ds(source, size), pl.ds(target, size)
            second.append(pltpu.make_async_copy(ref.at[here], terms.at[there], sems.at[1]))
    second = fetch(second)
    late[...] = jnp.zeros_like(late)
    held[pl.ds(nothing, block), :] = jnp.zeros((block, held.shape[1]), held.dtype)

    def clear(i, carry):
        counts[i] = 0
        for n in range(early):
            firsts[i, n] = nothing
            depths[i, n] = 0
        return carry

    lax.fori_loop(0, row_blocks + 1, clear, 0)
    for copy in first:
        copy.wait()
    for n in range(count):
        row = held[pl.ds(n * span + slots * block, PAD), :].astype(jnp.float32)
        code_rows[pl.ds(n, 1), :] = row[:1].astype(jnp.int32)
    to_scalars = pltpu.make_async_copy(code_rows, codes, sems.at[2])
    to_scalars.start()
    to_scalars.wait()
    my_row, my_col = spot[0], spot[1]

    def place(n, carry):
        col = my_col ^ offsets[n // grid_rows]
        source = (col // per_row) ^ my_row
        inner = col % per_row
        for j in range(slots):
            code = codes[n, j]
            row = code // panels
            k = (source * panels + code % panels) * per_row + inner
            record = pl.multiple_of(n * span + j * block, PAD)

            to = jnp.where((code >= 0) & (k < early), row, row_blocks)
            at = counts[to]
            firsts[to, jnp.minimum(at, early - 1)] = record
            depths[to, jnp.minimum(at, early - 1)] = k * block
            counts[to] = at + 1

            @pl.when((code >= 0) & (k >= early))
            def _():
                to = pl.ds(pl.multiple_of(row * block, block), block)
                late[k - early, to, :] = held[pl.ds(record, block), :]

        return carry

    lax.fori_loop(0, count, place, 0)
    for copy in second:
        copy.wait()

    def pair(i, n):
        def one(m):
            left = held[pl.ds(pl.multiple_of(firsts[i, m], PAD), block), :]
            right = terms[pl.ds(pl.multiple_of(depths[i, m], block), block), :]
            return left, right

        (left0, right0), (left1, right1) = one(2 * n), one(2 * n + 1)
        return jnp.dot(
            jnp.concatenate([left0, left1], axis=1),
            jnp.concatenate([right0, right1], axis=0),
            preferred_element_type=jnp.float32,
        )

    for i in range(row_blocks):
        rows = pl.ds(i * block, block)
        product = pair(i, 0) + pair(i, 1)
        acc[rows, :] = 2.0 * product

    def more(i, carry):
        rows = pl.ds(pl.multiple_of(i * block, block), block)

        def step(n, inner):
            acc[rows, :] += 2.0 * pair(i, n)
            return inner

        return lax.fori_loop(2, (counts[i] + 1) // 2, step, carry)

    lax.fori_loop(0, row_blocks, more, 0)


def late_kernel(dims, keep, acc, late, previous, *refs):
    block = dims[-1]
    term_refs, out, staged, sem = refs[:-3], *refs[-3:]
    blocks = late.shape[0]
    steps = acc.shape[0] // TILE
    right = jnp.concatenate([ref[...] for ref in term_refs], axis=0)
    copies = []
    for t in range(steps):
        rows = pl.ds(t * TILE, TILE)
        left = jnp.concatenate([late[k, rows, :] for k in range(blocks)], axis=1)
        product = jnp.dot(left, right, preferred_element_type=jnp.float32)
        update = acc[rows, :] + 2.0 * product - previous[rows, :].astype(jnp.float32)
        for i in range(TILE // block):
            for j in range(out.shape[1] // block):
                wanted = keep[t * (TILE // block) + i, j] > 0
                part = update[i * block : (i + 1) * block, j * block : (j + 1) * block]
                staged[pl.ds(t * TILE + i * block, block), pl.ds(j * block, block)] = jnp.where(
                    wanted, part, jnp.zeros_like(part)
                ).astype(out.dtype)
        copies.append(pltpu.make_async_copy(staged.at[rows], out.at[rows], sem))
        copies[-1].start()
    for copy in copies:
        copy.wait()


def per_device(send_blocks, send_count, send_place, term_current, term_previous, keep_mask):
    grid_rows, grid_cols = lax.axis_size("row"), lax.axis_size("col")
    my_row, my_col = lax.axis_index("row"), lax.axis_index("col")
    block = send_blocks.shape[-1]
    slots = send_blocks.shape[1]
    panels = term_current.shape[0]
    tile_rows, tile_cols = term_previous.shape
    row_blocks = tile_rows // block
    per_row = grid_cols // grid_rows
    dims = (grid_rows, grid_cols, slots, panels, block)

    lane = jnp.arange(slots, dtype=jnp.int32)
    places = jnp.where(lane[None, :] < send_count, send_place, -1).astype(jnp.bfloat16)
    pad = jnp.broadcast_to(
        jnp.pad(places, ((0, 0), (0, block - slots)))[:, None, :], (grid_rows, PAD, block)
    )

    def payload(offset):
        to = my_row ^ offset
        records = lax.dynamic_index_in_dim(send_blocks, to, 0, keepdims=False)
        tail = lax.dynamic_index_in_dim(pad, to, 0, keepdims=False)
        return jnp.concatenate([records.reshape(slots * block, block), tail], axis=0)

    got = [swap(payload(o), "row", o) for o in range(1, grid_rows)]

    last = grid_rows - 1
    rows = term_current.shape[1]
    flat = term_current.reshape(panels * rows, tile_cols)
    pieces = [(flat, [(0, 0, panels * rows)])]
    if grid_rows == 4 and panels == 2:
        size = panels * rows
        up, down = swap(flat, "row", 1), swap(flat, "row", 2)
        pieces += [(up, [(0, size, size)]), (down, [(0, 2 * size, size)])]
        final = [swap(up[:rows], "row", 2), swap(down[rows:], "row", 1)]
    else:
        for o in range(1, last):
            pieces.append((swap(flat, "row", o), [(0, o * panels * rows, panels * rows)]))
        final = [swap(flat[p * rows : (p + 1) * rows], "row", last) for p in range(panels)]

    own = jnp.concatenate([payload(0)] + got, axis=0)
    if grid_cols == 8:
        far, near = swap(own, "col", 6), swap(own, "col", 2)
        middle = swap(far, "col", 2)
        offsets = [0, 2, 6, 4]
        parts = [own, near, far, middle]
        groups = [jnp.concatenate(parts[:3], axis=0), middle]
        parts = groups
        others = [swap(group, "col", 1) for group in groups]
    else:
        offsets = list(range(0, grid_cols, 2))
        parts = [own] + [swap(own, "col", o) for o in offsets[1:]]
        others = [swap(part, "col", 1) for part in parts]
    offsets = offsets + [o ^ 1 for o in offsets]
    record_arrays = parts + others
    span = slots * block + PAD

    early = (grid_rows - 1) * panels * per_row
    anywhere = pl.BlockSpec(memory_space=pl.ANY)
    smem = pl.BlockSpec(memory_space=pltpu.SMEM)
    vmem = pl.BlockSpec(memory_space=pltpu.VMEM)
    late_blocks = panels * per_row
    count = grid_cols * grid_rows
    early_bytes = 2 * (early * block * tile_cols + count * span * block)
    passed_bytes = 4 * tile_rows * tile_cols + 2 * late_blocks * tile_rows * block
    acc, late = pl.pallas_call(
        functools.partial(early_kernel, dims, len(record_arrays), early, [p[1] for p in pieces]),
        out_shape=[
            jax.ShapeDtypeStruct((tile_rows, tile_cols), jnp.float32),
            jax.ShapeDtypeStruct((late_blocks, tile_rows, block), jnp.bfloat16),
        ],
        in_specs=[smem, smem] + [anywhere] * (len(record_arrays) + len(pieces)),
        out_specs=[vmem, vmem],
        scratch_shapes=[
            pltpu.VMEM((early * block, tile_cols), jnp.bfloat16),
            pltpu.VMEM((count * span + block, block), jnp.bfloat16),
            pltpu.VMEM((count, block), jnp.int32),
            pltpu.SMEM((count, block), jnp.int32),
            pltpu.SMEM((row_blocks + 1,), jnp.int32),
            pltpu.SMEM((row_blocks + 1, early), jnp.int32),
            pltpu.SMEM((row_blocks + 1, early), jnp.int32),
            pltpu.SemaphoreType.DMA((3,)),
        ],
        compiler_params=pltpu.CompilerParams(vmem_limit_bytes=early_bytes + passed_bytes + SLACK),
        name="early_product",
    )(
        jnp.stack([my_row, my_col]).astype(jnp.int32),
        jnp.array(offsets, jnp.int32),
        *record_arrays,
        *[p[0] for p in pieces],
    )
    return pl.pallas_call(
        functools.partial(late_kernel, dims),
        out_shape=jax.ShapeDtypeStruct((tile_rows, tile_cols), term_previous.dtype),
        in_specs=[smem, vmem, vmem, vmem] + [vmem] * len(final),
        out_specs=anywhere,
        scratch_shapes=[
            pltpu.VMEM((tile_rows, tile_cols), term_previous.dtype),
            pltpu.SemaphoreType.DMA,
        ],
        compiler_params=pltpu.CompilerParams(vmem_limit_bytes=passed_bytes + 4 * tile_rows * tile_cols + SLACK),
        name="late_product",
    )(keep_mask, acc, late, term_previous, *final)


def solution(mesh):
    placed = (
        P("row", "col", None, None),
        P("row", "col"),
        P("row", "col"),
        P(None, "row", "col"),
        P("row", "col"),
        P("row", "col"),
    )
    return jax.shard_map(
        per_device, mesh=mesh, in_specs=placed, out_specs=P("row", "col"), check_vma=False
    )
```

```python
import functools

import jax
import jax.numpy as jnp
from jax import lax
from jax.experimental import pallas as pl
from jax.experimental.pallas import tpu as pltpu
from jax.sharding import PartitionSpec as P

SMALL = 1024 * 1024
SLACK = 5 * 1024 * 1024
PAD = 16
TILE = 256


def swap(x, axis, offset):
    size = lax.axis_size(axis)
    return lax.ppermute(x, axis, [(i, i ^ offset) for i in range(size)])


def join_kernel(*refs):
    parts, out, sems = refs[:-2], refs[-2], refs[-1]
    copies, at = [], 0
    for n, part in enumerate(parts):
        rows = pl.ds(at, part.shape[0])
        copies.append(pltpu.make_async_copy(part, out.at[rows], sems.at[n]))
        copies[-1].start()
        at += part.shape[0]
    for copy in copies:
        copy.wait()


def join(parts):
    rows = sum(part.shape[0] for part in parts)
    return pl.pallas_call(
        join_kernel,
        out_shape=jax.ShapeDtypeStruct((rows, parts[0].shape[1]), parts[0].dtype),
        in_specs=[pl.BlockSpec(memory_space=pl.ANY)] * len(parts),
        out_specs=pl.BlockSpec(memory_space=pl.ANY),
        scratch_shapes=[pltpu.SemaphoreType.DMA((len(parts),))],
        compiler_params=pltpu.CompilerParams(vmem_limit_bytes=SMALL),
        name="join",
    )(*parts)


def hold_kernel(*refs):
    pass


def hold(array, others):
    return pl.pallas_call(
        hold_kernel,
        out_shape=jax.ShapeDtypeStruct(array.shape, array.dtype),
        in_specs=[pl.BlockSpec(memory_space=pl.ANY)] * (1 + len(others)),
        out_specs=pl.BlockSpec(memory_space=pl.ANY),
        input_output_aliases={0: 0},
        compiler_params=pltpu.CompilerParams(vmem_limit_bytes=SMALL),
        name="hold",
    )(array, *others)


def early_kernel(dims, arrays, early, routes, spot, offsets, *refs):
    grid_rows, grid_cols, slots, panels, block = dims
    span = slots * block + PAD
    per_row = grid_cols // grid_rows
    record_refs = refs[:arrays]
    term_refs = refs[arrays:-10]
    acc, late, terms, held, code_rows, codes, counts, firsts, depths, sems = refs[-10:]
    row_blocks = acc.shape[0] // block
    count = grid_rows * grid_cols
    nothing = count * span

    def fetch(copies):
        for copy in copies:
            copy.start()
        return copies

    at, first = 0, []
    for ref in record_refs:
        rows = pl.ds(at, ref.shape[0])
        first.append(pltpu.make_async_copy(ref, held.at[rows], sems.at[0]))
        at += ref.shape[0]
    first = fetch(first)
    second = []
    for ref, route in zip(term_refs, routes):
        for source, target, size in route:
            here, there = pl.ds(source, size), pl.ds(target, size)
            second.append(pltpu.make_async_copy(ref.at[here], terms.at[there], sems.at[1]))
    second = fetch(second)
    late[...] = jnp.zeros_like(late)
    held[pl.ds(nothing, block), :] = jnp.zeros((block, held.shape[1]), held.dtype)

    def clear(i, carry):
        counts[i] = 0
        for n in range(early):
            firsts[i, n] = nothing
            depths[i, n] = 0
        return carry

    lax.fori_loop(0, row_blocks + 1, clear, 0)
    for copy in first:
        copy.wait()
    for n in range(count):
        row = held[pl.ds(n * span + slots * block, PAD), :].astype(jnp.float32)
        code_rows[pl.ds(n, 1), :] = row[:1].astype(jnp.int32)
    to_scalars = pltpu.make_async_copy(code_rows, codes, sems.at[2])
    to_scalars.start()
    to_scalars.wait()
    my_row, my_col = spot[0], spot[1]

    def place(n, carry):
        col = my_col ^ offsets[n // grid_rows]
        source = (col // per_row) ^ my_row
        inner = col % per_row
        for j in range(slots):
            code = codes[n, j]
            row = code // panels
            k = (source * panels + code % panels) * per_row + inner
            record = pl.multiple_of(n * span + j * block, PAD)

            to = jnp.where((code >= 0) & (k < early), row, row_blocks)
            at = counts[to]
            firsts[to, jnp.minimum(at, early - 1)] = record
            depths[to, jnp.minimum(at, early - 1)] = k * block
            counts[to] = at + 1

            @pl.when((code >= 0) & (k >= early))
            def _():
                to = pl.ds(pl.multiple_of(row * block, block), block)
                late[k - early, to, :] = held[pl.ds(record, block), :]

        return carry

    lax.fori_loop(0, count, place, 0)
    for copy in second:
        copy.wait()

    def pair(i, n):
        def one(m):
            left = held[pl.ds(pl.multiple_of(firsts[i, m], PAD), block), :]
            right = terms[pl.ds(pl.multiple_of(depths[i, m], block), block), :]
            return left, right

        (left0, right0), (left1, right1) = one(2 * n), one(2 * n + 1)
        return jnp.dot(
            jnp.concatenate([left0, left1], axis=1),
            jnp.concatenate([right0, right1], axis=0),
            preferred_element_type=jnp.float32,
        )

    for i in range(row_blocks):
        rows = pl.ds(i * block, block)
        product = pair(i, 0) + pair(i, 1)
        acc[rows, :] = 2.0 * product

    def more(i, carry):
        rows = pl.ds(pl.multiple_of(i * block, block), block)

        def step(n, inner):
            acc[rows, :] += 2.0 * pair(i, n)
            return inner

        return lax.fori_loop(2, (counts[i] + 1) // 2, step, carry)

    lax.fori_loop(0, row_blocks, more, 0)


def late_kernel(dims, keep, acc, late, previous, *refs):
    block = dims[-1]
    term_refs, out, staged, sem = refs[:-3], *refs[-3:]
    blocks = late.shape[0]
    steps = acc.shape[0] // TILE
    right = jnp.concatenate([ref[...] for ref in term_refs], axis=0)
    copies = []
    for t in range(steps):
        rows = pl.ds(t * TILE, TILE)
        left = jnp.concatenate([late[k, rows, :] for k in range(blocks)], axis=1)
        product = jnp.dot(left, right, preferred_element_type=jnp.float32)
        update = acc[rows, :] + 2.0 * product - previous[rows, :].astype(jnp.float32)
        for i in range(TILE // block):
            for j in range(out.shape[1] // block):
                wanted = keep[t * (TILE // block) + i, j] > 0
                part = update[i * block : (i + 1) * block, j * block : (j + 1) * block]
                staged[pl.ds(t * TILE + i * block, block), pl.ds(j * block, block)] = jnp.where(
                    wanted, part, jnp.zeros_like(part)
                ).astype(out.dtype)
        copies.append(pltpu.make_async_copy(staged.at[rows], out.at[rows], sem))
        copies[-1].start()
    for copy in copies:
        copy.wait()


def per_device(send_blocks, send_count, send_place, term_current, term_previous, keep_mask):
    grid_rows, grid_cols = lax.axis_size("row"), lax.axis_size("col")
    my_row, my_col = lax.axis_index("row"), lax.axis_index("col")
    block = send_blocks.shape[-1]
    slots = send_blocks.shape[1]
    panels = term_current.shape[0]
    tile_rows, tile_cols = term_previous.shape
    row_blocks = tile_rows // block
    per_row = grid_cols // grid_rows
    dims = (grid_rows, grid_cols, slots, panels, block)

    lane = jnp.arange(slots, dtype=jnp.int32)
    places = jnp.where(lane[None, :] < send_count, send_place, -1).astype(jnp.bfloat16)
    pad = jnp.broadcast_to(
        jnp.pad(places, ((0, 0), (0, block - slots)))[:, None, :], (grid_rows, PAD, block)
    )

    def payload(offset):
        to = my_row ^ offset
        records = lax.dynamic_index_in_dim(send_blocks, to, 0, keepdims=False)
        tail = lax.dynamic_index_in_dim(pad, to, 0, keepdims=False)
        return jnp.concatenate([records.reshape(slots * block, block), tail], axis=0)

    got = [swap(payload(o), "row", o) for o in range(1, grid_rows)]

    last = grid_rows - 1
    rows = term_current.shape[1]
    flat = term_current.reshape(panels * rows, tile_cols)
    pieces = [(flat, [(0, 0, panels * rows)])]
    if grid_rows == 4 and panels == 2:
        size = panels * rows
        flat = hold(flat, got)
        up, down = swap(flat, "row", 1), swap(flat, "row", 2)
        pieces += [(up, [(0, size, size)]), (down, [(0, 2 * size, size)])]
        final = [swap(up[:rows], "row", 2), swap(down[rows:], "row", 1)]
    else:
        for o in range(1, last):
            pieces.append((swap(flat, "row", o), [(0, o * panels * rows, panels * rows)]))
        final = [swap(flat[p * rows : (p + 1) * rows], "row", last) for p in range(panels)]

    own = join([payload(0)] + got)
    if grid_cols == 8:
        far, near = swap(own, "col", 6), swap(own, "col", 2)
        middle = swap(far, "col", 2)
        offsets = [0, 6, 2, 4]
        groups = [jnp.concatenate([own, far], axis=0), near, middle]
        parts = groups
        others = [swap(group, "col", 1) for group in groups]
    else:
        offsets = list(range(0, grid_cols, 2))
        parts = [own] + [swap(own, "col", o) for o in offsets[1:]]
        others = [swap(part, "col", 1) for part in parts]
    offsets = offsets + [o ^ 1 for o in offsets]
    record_arrays = parts + others
    span = slots * block + PAD

    early = (grid_rows - 1) * panels * per_row
    anywhere = pl.BlockSpec(memory_space=pl.ANY)
    smem = pl.BlockSpec(memory_space=pltpu.SMEM)
    vmem = pl.BlockSpec(memory_space=pltpu.VMEM)
    late_blocks = panels * per_row
    count = grid_cols * grid_rows
    early_bytes = 2 * (early * block * tile_cols + count * span * block)
    passed_bytes = 4 * tile_rows * tile_cols + 2 * late_blocks * tile_rows * block
    acc, late = pl.pallas_call(
        functools.partial(early_kernel, dims, len(record_arrays), early, [p[1] for p in pieces]),
        out_shape=[
            jax.ShapeDtypeStruct((tile_rows, tile_cols), jnp.float32),
            jax.ShapeDtypeStruct((late_blocks, tile_rows, block), jnp.bfloat16),
        ],
        in_specs=[smem, smem] + [anywhere] * (len(record_arrays) + len(pieces)),
        out_specs=[vmem, vmem],
        scratch_shapes=[
            pltpu.VMEM((early * block, tile_cols), jnp.bfloat16),
            pltpu.VMEM((count * span + block, block), jnp.bfloat16),
            pltpu.VMEM((count, block), jnp.int32),
            pltpu.SMEM((count, block), jnp.int32),
            pltpu.SMEM((row_blocks + 1,), jnp.int32),
            pltpu.SMEM((row_blocks + 1, early), jnp.int32),
            pltpu.SMEM((row_blocks + 1, early), jnp.int32),
            pltpu.SemaphoreType.DMA((3,)),
        ],
        compiler_params=pltpu.CompilerParams(vmem_limit_bytes=early_bytes + passed_bytes + SLACK),
        name="early_product",
    )(
        jnp.stack([my_row, my_col]).astype(jnp.int32),
        jnp.array(offsets, jnp.int32),
        *record_arrays,
        *[p[0] for p in pieces],
    )
    return pl.pallas_call(
        functools.partial(late_kernel, dims),
        out_shape=jax.ShapeDtypeStruct((tile_rows, tile_cols), term_previous.dtype),
        in_specs=[smem, vmem, vmem, vmem] + [vmem] * len(final),
        out_specs=anywhere,
        scratch_shapes=[
            pltpu.VMEM((tile_rows, tile_cols), term_previous.dtype),
            pltpu.SemaphoreType.DMA,
        ],
        compiler_params=pltpu.CompilerParams(vmem_limit_bytes=passed_bytes + 4 * tile_rows * tile_cols + SLACK),
        name="late_product",
    )(keep_mask, acc, late, term_previous, *final)


def solution(mesh):
    placed = (
        P("row", "col", None, None),
        P("row", "col"),
        P("row", "col"),
        P(None, "row", "col"),
        P("row", "col"),
        P("row", "col"),
    )
    return jax.shard_map(
        per_device, mesh=mesh, in_specs=placed, out_specs=P("row", "col"), check_vma=False
    )
```

```python
import functools

import jax
import jax.numpy as jnp
from jax import lax
from jax.experimental import pallas as pl
from jax.experimental.pallas import tpu as pltpu
from jax.sharding import PartitionSpec as P

SMALL = 1024 * 1024
SLACK = 5 * 1024 * 1024
PAD = 16
TILE = 256


def swap(x, axis, offset):
    size = lax.axis_size(axis)
    return lax.ppermute(x, axis, [(i, i ^ offset) for i in range(size)])


def join_kernel(*refs):
    parts, out, sems = refs[:-2], refs[-2], refs[-1]
    copies, at = [], 0
    for n, part in enumerate(parts):
        rows = pl.ds(at, part.shape[0])
        copies.append(pltpu.make_async_copy(part, out.at[rows], sems.at[n]))
        copies[-1].start()
        at += part.shape[0]
    for copy in copies:
        copy.wait()


def join(parts):
    rows = sum(part.shape[0] for part in parts)
    return pl.pallas_call(
        join_kernel,
        out_shape=jax.ShapeDtypeStruct((rows, parts[0].shape[1]), parts[0].dtype),
        in_specs=[pl.BlockSpec(memory_space=pl.ANY)] * len(parts),
        out_specs=pl.BlockSpec(memory_space=pl.ANY),
        scratch_shapes=[pltpu.SemaphoreType.DMA((len(parts),))],
        compiler_params=pltpu.CompilerParams(vmem_limit_bytes=SMALL),
        name="join",
    )(*parts)


def hold_kernel(*refs):
    pass


def hold(array, others):
    return pl.pallas_call(
        hold_kernel,
        out_shape=jax.ShapeDtypeStruct(array.shape, array.dtype),
        in_specs=[pl.BlockSpec(memory_space=pl.ANY)] * (1 + len(others)),
        out_specs=pl.BlockSpec(memory_space=pl.ANY),
        input_output_aliases={0: 0},
        compiler_params=pltpu.CompilerParams(vmem_limit_bytes=SMALL),
        name="hold",
    )(array, *others)


def split(number, size):
    if size & (size - 1) == 0:
        return number >> (size.bit_length() - 1), number & (size - 1)
    return number // size, number % size


def early_kernel(dims, arrays, early, routes, spot, offsets, *refs):
    grid_rows, grid_cols, slots, panels, block = dims
    span = slots * block + PAD
    per_row = grid_cols // grid_rows
    record_refs = refs[:arrays]
    term_refs = refs[arrays:-10]
    acc, late, terms, held, code_rows, codes, counts, firsts, depths, sems = refs[-10:]
    row_blocks = acc.shape[0] // block
    count = grid_rows * grid_cols
    nothing = count * span

    def fetch(copies):
        for copy in copies:
            copy.start()
        return copies

    at, first = 0, []
    for ref in record_refs:
        rows = pl.ds(at, ref.shape[0])
        first.append(pltpu.make_async_copy(ref, held.at[rows], sems.at[0]))
        at += ref.shape[0]
    first = fetch(first)
    second = []
    for ref, route in zip(term_refs, routes):
        for source, target, size in route:
            here, there = pl.ds(source, size), pl.ds(target, size)
            second.append(pltpu.make_async_copy(ref.at[here], terms.at[there], sems.at[1]))
    second = fetch(second)
    late[...] = jnp.zeros_like(late)
    held[pl.ds(nothing, block), :] = jnp.zeros((block, held.shape[1]), held.dtype)

    def clear(i, carry):
        counts[i] = 0
        for n in range(early):
            firsts[i, n] = nothing
            depths[i, n] = 0
        return carry

    lax.fori_loop(0, row_blocks + 1, clear, 0, unroll=True)
    for copy in first:
        copy.wait()
    for n in range(count):
        row = held[pl.ds(n * span + slots * block, PAD), :].astype(jnp.float32)
        code_rows[pl.ds(n, 1), :] = row[:1].astype(jnp.int32)
    to_scalars = pltpu.make_async_copy(code_rows, codes, sems.at[2])
    to_scalars.start()
    to_scalars.wait()
    my_row, my_col = spot[0], spot[1]

    def place(n, carry):
        source, inner = split(my_col ^ offsets[split(n, grid_rows)[0]], per_row)
        source = source ^ my_row
        for j in range(slots):
            code = codes[n, j]
            row, panel = split(code, panels)
            k = (source * panels + panel) * per_row + inner
            record = pl.multiple_of(n * span + j * block, PAD)

            to = jnp.where((code >= 0) & (k < early), row, row_blocks)
            at = counts[to]
            firsts[to, jnp.minimum(at, early - 1)] = record
            depths[to, jnp.minimum(at, early - 1)] = k * block
            counts[to] = at + 1

            @pl.when((code >= 0) & (k >= early))
            def _():
                to = pl.ds(pl.multiple_of(row * block, block), block)
                late[k - early, to, :] = held[pl.ds(record, block), :]

        return carry

    lax.fori_loop(0, count, place, 0, unroll=4)
    for copy in second:
        copy.wait()

    def pair(i, n):
        def one(m):
            left = held[pl.ds(pl.multiple_of(firsts[i, m], PAD), block), :]
            right = terms[pl.ds(pl.multiple_of(depths[i, m], block), block), :]
            return left, right

        (left0, right0), (left1, right1) = one(2 * n), one(2 * n + 1)
        return jnp.dot(
            jnp.concatenate([left0, left1], axis=1),
            jnp.concatenate([right0, right1], axis=0),
            preferred_element_type=jnp.float32,
        )

    for i in range(row_blocks):
        rows = pl.ds(i * block, block)
        product = pair(i, 0) + pair(i, 1)
        acc[rows, :] = 2.0 * product

    def more(i, carry):
        rows = pl.ds(pl.multiple_of(i * block, block), block)

        def step(n, inner):
            acc[rows, :] += 2.0 * pair(i, n)
            return inner

        return lax.fori_loop(2, (counts[i] + 1) >> 1, step, carry)

    lax.fori_loop(0, row_blocks, more, 0)


def late_kernel(dims, keep, acc, late, previous, *refs):
    block = dims[-1]
    term_refs, out, staged, sem = refs[:-3], *refs[-3:]
    blocks = late.shape[0]
    steps = acc.shape[0] // TILE
    right = jnp.concatenate([ref[...] for ref in term_refs], axis=0)
    copies = []
    for t in range(steps):
        rows = pl.ds(t * TILE, TILE)
        left = jnp.concatenate([late[k, rows, :] for k in range(blocks)], axis=1)
        product = jnp.dot(left, right, preferred_element_type=jnp.float32)
        update = acc[rows, :] + 2.0 * product - previous[rows, :].astype(jnp.float32)
        for i in range(TILE // block):
            for j in range(out.shape[1] // block):
                wanted = keep[t * (TILE // block) + i, j] > 0
                part = update[i * block : (i + 1) * block, j * block : (j + 1) * block]
                staged[pl.ds(t * TILE + i * block, block), pl.ds(j * block, block)] = jnp.where(
                    wanted, part, jnp.zeros_like(part)
                ).astype(out.dtype)
        copies.append(pltpu.make_async_copy(staged.at[rows], out.at[rows], sem))
        copies[-1].start()
    for copy in copies:
        copy.wait()


def per_device(send_blocks, send_count, send_place, term_current, term_previous, keep_mask):
    grid_rows, grid_cols = lax.axis_size("row"), lax.axis_size("col")
    my_row, my_col = lax.axis_index("row"), lax.axis_index("col")
    block = send_blocks.shape[-1]
    slots = send_blocks.shape[1]
    panels = term_current.shape[0]
    tile_rows, tile_cols = term_previous.shape
    row_blocks = tile_rows // block
    per_row = grid_cols // grid_rows
    dims = (grid_rows, grid_cols, slots, panels, block)

    lane = jnp.arange(slots, dtype=jnp.int32)
    places = jnp.where(lane[None, :] < send_count, send_place, -1).astype(jnp.bfloat16)
    pad = jnp.broadcast_to(
        jnp.pad(places, ((0, 0), (0, block - slots)))[:, None, :], (grid_rows, PAD, block)
    )

    def payload(offset):
        to = my_row ^ offset
        records = lax.dynamic_index_in_dim(send_blocks, to, 0, keepdims=False)
        tail = lax.dynamic_index_in_dim(pad, to, 0, keepdims=False)
        return jnp.concatenate([records.reshape(slots * block, block), tail], axis=0)

    got = [swap(payload(o), "row", o) for o in range(1, grid_rows)]

    last = grid_rows - 1
    rows = term_current.shape[1]
    flat = term_current.reshape(panels * rows, tile_cols)
    pieces = [(flat, [(0, 0, panels * rows)])]
    if grid_rows == 4 and panels == 2:
        size = panels * rows
        flat = hold(flat, got)
        up, down = swap(flat, "row", 1), swap(flat, "row", 2)
        pieces += [(up, [(0, size, size)]), (down, [(0, 2 * size, size)])]
        final = [swap(up[:rows], "row", 2), swap(down[rows:], "row", 1)]
    else:
        for o in range(1, last):
            pieces.append((swap(flat, "row", o), [(0, o * panels * rows, panels * rows)]))
        final = [swap(flat[p * rows : (p + 1) * rows], "row", last) for p in range(panels)]

    own = join([payload(0)] + got)
    if grid_cols == 8:
        far, near = swap(own, "col", 6), swap(own, "col", 2)
        middle = swap(far, "col", 2)
        offsets = [0, 6, 2, 4]
        groups = [jnp.concatenate([own, far], axis=0), near, middle]
        parts = groups
        others = [swap(group, "col", 1) for group in groups]
    else:
        offsets = list(range(0, grid_cols, 2))
        parts = [own] + [swap(own, "col", o) for o in offsets[1:]]
        others = [swap(part, "col", 1) for part in parts]
    offsets = offsets + [o ^ 1 for o in offsets]
    record_arrays = parts + others
    span = slots * block + PAD

    early = (grid_rows - 1) * panels * per_row
    anywhere = pl.BlockSpec(memory_space=pl.ANY)
    smem = pl.BlockSpec(memory_space=pltpu.SMEM)
    vmem = pl.BlockSpec(memory_space=pltpu.VMEM)
    late_blocks = panels * per_row
    count = grid_cols * grid_rows
    early_bytes = 2 * (early * block * tile_cols + count * span * block)
    passed_bytes = 4 * tile_rows * tile_cols + 2 * late_blocks * tile_rows * block
    acc, late = pl.pallas_call(
        functools.partial(early_kernel, dims, len(record_arrays), early, [p[1] for p in pieces]),
        out_shape=[
            jax.ShapeDtypeStruct((tile_rows, tile_cols), jnp.float32),
            jax.ShapeDtypeStruct((late_blocks, tile_rows, block), jnp.bfloat16),
        ],
        in_specs=[smem, smem] + [anywhere] * (len(record_arrays) + len(pieces)),
        out_specs=[vmem, vmem],
        scratch_shapes=[
            pltpu.VMEM((early * block, tile_cols), jnp.bfloat16),
            pltpu.VMEM((count * span + block, block), jnp.bfloat16),
            pltpu.VMEM((count, block), jnp.int32),
            pltpu.SMEM((count, block), jnp.int32),
            pltpu.SMEM((row_blocks + 1,), jnp.int32),
            pltpu.SMEM((row_blocks + 1, early), jnp.int32),
            pltpu.SMEM((row_blocks + 1, early), jnp.int32),
            pltpu.SemaphoreType.DMA((3,)),
        ],
        compiler_params=pltpu.CompilerParams(vmem_limit_bytes=early_bytes + passed_bytes + SLACK),
        name="early_product",
    )(
        jnp.stack([my_row, my_col]).astype(jnp.int32),
        jnp.array(offsets, jnp.int32),
        *record_arrays,
        *[p[0] for p in pieces],
    )
    return pl.pallas_call(
        functools.partial(late_kernel, dims),
        out_shape=jax.ShapeDtypeStruct((tile_rows, tile_cols), term_previous.dtype),
        in_specs=[smem, vmem, vmem, vmem] + [vmem] * len(final),
        out_specs=anywhere,
        scratch_shapes=[
            pltpu.VMEM((tile_rows, tile_cols), term_previous.dtype),
            pltpu.SemaphoreType.DMA,
        ],
        compiler_params=pltpu.CompilerParams(vmem_limit_bytes=passed_bytes + 4 * tile_rows * tile_cols + SLACK),
        name="late_product",
    )(keep_mask, acc, late, term_previous, *final)


def solution(mesh):
    placed = (
        P("row", "col", None, None),
        P("row", "col"),
        P("row", "col"),
        P(None, "row", "col"),
        P("row", "col"),
        P("row", "col"),
    )
    return jax.shard_map(
        per_device, mesh=mesh, in_specs=placed, out_specs=P("row", "col"), check_vma=False
    )
```

```python
import functools

import jax
import jax.numpy as jnp
from jax import lax
from jax.experimental import pallas as pl
from jax.experimental.pallas import tpu as pltpu
from jax.sharding import PartitionSpec as P

SMALL = 1024 * 1024
SLACK = 5 * 1024 * 1024
PAD = 16
TILE = 256


def swap(x, axis, offset):
    size = lax.axis_size(axis)
    return lax.ppermute(x, axis, [(i, i ^ offset) for i in range(size)])


def join_kernel(*refs):
    parts, out, sems = refs[:-2], refs[-2], refs[-1]
    copies, at = [], 0
    for n, part in enumerate(parts):
        rows = pl.ds(at, part.shape[0])
        copies.append(pltpu.make_async_copy(part, out.at[rows], sems.at[n]))
        copies[-1].start()
        at += part.shape[0]
    for copy in copies:
        copy.wait()


def join(parts):
    rows = sum(part.shape[0] for part in parts)
    return pl.pallas_call(
        join_kernel,
        out_shape=jax.ShapeDtypeStruct((rows, parts[0].shape[1]), parts[0].dtype),
        in_specs=[pl.BlockSpec(memory_space=pl.ANY)] * len(parts),
        out_specs=pl.BlockSpec(memory_space=pl.ANY),
        scratch_shapes=[pltpu.SemaphoreType.DMA((len(parts),))],
        compiler_params=pltpu.CompilerParams(vmem_limit_bytes=SMALL),
        name="join",
    )(*parts)


def hold_kernel(*refs):
    pass


def hold(array, others):
    return pl.pallas_call(
        hold_kernel,
        out_shape=jax.ShapeDtypeStruct(array.shape, array.dtype),
        in_specs=[pl.BlockSpec(memory_space=pl.ANY)] * (1 + len(others)),
        out_specs=pl.BlockSpec(memory_space=pl.ANY),
        input_output_aliases={0: 0},
        compiler_params=pltpu.CompilerParams(vmem_limit_bytes=SMALL),
        name="hold",
    )(array, *others)


def split(number, size):
    if size & (size - 1) == 0:
        return number >> (size.bit_length() - 1), number & (size - 1)
    return number // size, number % size


def early_kernel(dims, arrays, early, routes, spot, offsets, *refs):
    grid_rows, grid_cols, slots, panels, block = dims
    span = slots * block + PAD
    per_row = grid_cols // grid_rows
    record_refs = refs[:arrays]
    term_refs = refs[arrays:-10]
    acc, late, terms, held, code_rows, codes, counts, firsts, depths, sems = refs[-10:]
    row_blocks = acc.shape[0] // block
    count = grid_rows * grid_cols
    nothing = count * span

    def fetch(copies):
        for copy in copies:
            copy.start()
        return copies

    at, first = 0, []
    for ref in record_refs:
        rows = pl.ds(at, ref.shape[0])
        first.append(pltpu.make_async_copy(ref, held.at[rows], sems.at[0]))
        at += ref.shape[0]
    first = fetch(first)
    second = []
    for ref, route in zip(term_refs, routes):
        for source, target, size in route:
            here, there = pl.ds(source, size), pl.ds(target, size)
            second.append(pltpu.make_async_copy(ref.at[here], terms.at[there], sems.at[1]))
    second = fetch(second)
    late[...] = jnp.zeros_like(late)
    held[pl.ds(nothing, block), :] = jnp.zeros((block, held.shape[1]), held.dtype)

    def clear(i, carry):
        counts[i] = 0
        for n in range(early):
            firsts[i, n] = nothing
            depths[i, n] = 0
        return carry

    lax.fori_loop(0, row_blocks + 1, clear, 0, unroll=True)
    for copy in first:
        copy.wait()
    for n in range(count):
        row = held[pl.ds(n * span + slots * block, PAD), :].astype(jnp.float32)
        code_rows[pl.ds(n, 1), :] = row[:1].astype(jnp.int32)
    to_scalars = pltpu.make_async_copy(code_rows, codes, sems.at[2])
    to_scalars.start()
    to_scalars.wait()
    my_row, my_col = spot[0], spot[1]

    def place(n, carry):
        source, inner = split(my_col ^ offsets[split(n, grid_rows)[0]], per_row)
        source = source ^ my_row
        for j in range(slots):
            code = codes[n, j]
            row, panel = split(code, panels)
            k = (source * panels + panel) * per_row + inner
            record = pl.multiple_of(n * span + j * block, PAD)

            to = jnp.where((code >= 0) & (k < early), row, row_blocks)
            at = counts[to]
            firsts[to, jnp.minimum(at, early - 1)] = record
            depths[to, jnp.minimum(at, early - 1)] = k * block
            counts[to] = at + 1

            @pl.when((code >= 0) & (k >= early))
            def _():
                to = pl.ds(pl.multiple_of(row * block, block), block)
                late[k - early, to, :] = held[pl.ds(record, block), :]

        return carry

    lax.fori_loop(0, count, place, 0, unroll=4)
    for copy in second:
        copy.wait()

    def pair(i, n):
        def one(m):
            left = held[pl.ds(pl.multiple_of(firsts[i, m], PAD), block), :]
            right = terms[pl.ds(pl.multiple_of(depths[i, m], block), block), :]
            return left, right

        (left0, right0), (left1, right1) = one(2 * n), one(2 * n + 1)
        return jnp.dot(
            jnp.concatenate([left0, left1], axis=1),
            jnp.concatenate([right0, right1], axis=0),
            preferred_element_type=jnp.float32,
        )

    for i in range(row_blocks):
        rows = pl.ds(i * block, block)
        product = pair(i, 0) + pair(i, 1)
        acc[rows, :] = 2.0 * product

    def more(i, carry):
        rows = pl.ds(pl.multiple_of(i * block, block), block)

        def step(n, inner):
            acc[rows, :] += 2.0 * pair(i, n)
            return inner

        return lax.fori_loop(2, (counts[i] + 1) >> 1, step, carry)

    lax.fori_loop(0, row_blocks, more, 0)


def late_kernel(dims, keep, acc, late, previous, *refs):
    block = dims[-1]
    term_refs, out, staged, sem = refs[:-3], *refs[-3:]
    blocks = late.shape[0]
    steps = acc.shape[0] // TILE
    right = jnp.concatenate([ref[...] for ref in term_refs], axis=0)
    copies = []
    for t in range(steps):
        rows = pl.ds(t * TILE, TILE)
        left = jnp.concatenate([late[k, rows, :] for k in range(blocks)], axis=1)
        product = jnp.dot(left, right, preferred_element_type=jnp.float32)
        update = acc[rows, :] + 2.0 * product - previous[rows, :].astype(jnp.float32)
        for i in range(TILE // block):
            for j in range(out.shape[1] // block):
                wanted = keep[t * (TILE // block) + i, j] > 0
                part = update[i * block : (i + 1) * block, j * block : (j + 1) * block]
                staged[pl.ds(t * TILE + i * block, block), pl.ds(j * block, block)] = jnp.where(
                    wanted, part, jnp.zeros_like(part)
                ).astype(out.dtype)
        copies.append(pltpu.make_async_copy(staged.at[rows], out.at[rows], sem))
        copies[-1].start()
    for copy in copies:
        copy.wait()


def per_device(send_blocks, send_count, send_place, term_current, term_previous, keep_mask):
    grid_rows, grid_cols = lax.axis_size("row"), lax.axis_size("col")
    my_row, my_col = lax.axis_index("row"), lax.axis_index("col")
    block = send_blocks.shape[-1]
    slots = send_blocks.shape[1]
    panels = term_current.shape[0]
    tile_rows, tile_cols = term_previous.shape
    row_blocks = tile_rows // block
    per_row = grid_cols // grid_rows
    dims = (grid_rows, grid_cols, slots, panels, block)

    lane = jnp.arange(slots, dtype=jnp.int32)
    places = jnp.where(lane[None, :] < send_count, send_place, -1).astype(jnp.bfloat16)
    pad = jnp.broadcast_to(
        jnp.pad(places, ((0, 0), (0, block - slots)))[:, None, :], (grid_rows, PAD, block)
    )

    def payload(offset):
        to = my_row ^ offset
        records = lax.dynamic_index_in_dim(send_blocks, to, 0, keepdims=False)
        tail = lax.dynamic_index_in_dim(pad, to, 0, keepdims=False)
        return jnp.concatenate([records.reshape(slots * block, block), tail], axis=0)

    got = [swap(payload(o), "row", o) for o in range(1, grid_rows)]

    last = grid_rows - 1
    rows = term_current.shape[1]
    flat = term_current.reshape(panels * rows, tile_cols)
    pieces = [(flat, [(0, 0, panels * rows)])]
    if grid_rows == 4 and panels == 2:
        size = panels * rows
        flat = hold(flat, got)
        up, down = swap(flat, "row", 1), swap(flat, "row", 2)
        pieces += [(up, [(0, size, size)]), (down, [(0, 2 * size, size)])]
        at = rows + PAD
        final = [swap(up[:at], "row", 2), swap(down[at:], "row", 1)]
    else:
        for o in range(1, last):
            pieces.append((swap(flat, "row", o), [(0, o * panels * rows, panels * rows)]))
        final = [swap(flat[p * rows : (p + 1) * rows], "row", last) for p in range(panels)]

    own = join([payload(0)] + got)
    if grid_cols == 8:
        far, near = swap(own, "col", 6), swap(own, "col", 2)
        middle = swap(far, "col", 2)
        offsets = [0, 6, 2, 4]
        groups = [jnp.concatenate([own, far], axis=0), near, middle]
        parts = groups
        others = [swap(group, "col", 1) for group in groups]
    else:
        offsets = list(range(0, grid_cols, 2))
        parts = [own] + [swap(own, "col", o) for o in offsets[1:]]
        others = [swap(part, "col", 1) for part in parts]
    offsets = offsets + [o ^ 1 for o in offsets]
    record_arrays = parts + others
    span = slots * block + PAD

    early = (grid_rows - 1) * panels * per_row
    anywhere = pl.BlockSpec(memory_space=pl.ANY)
    smem = pl.BlockSpec(memory_space=pltpu.SMEM)
    vmem = pl.BlockSpec(memory_space=pltpu.VMEM)
    late_blocks = panels * per_row
    count = grid_cols * grid_rows
    early_bytes = 2 * (early * block * tile_cols + count * span * block)
    passed_bytes = 4 * tile_rows * tile_cols + 2 * late_blocks * tile_rows * block
    acc, late = pl.pallas_call(
        functools.partial(early_kernel, dims, len(record_arrays), early, [p[1] for p in pieces]),
        out_shape=[
            jax.ShapeDtypeStruct((tile_rows, tile_cols), jnp.float32),
            jax.ShapeDtypeStruct((late_blocks, tile_rows, block), jnp.bfloat16),
        ],
        in_specs=[smem, smem] + [anywhere] * (len(record_arrays) + len(pieces)),
        out_specs=[vmem, vmem],
        scratch_shapes=[
            pltpu.VMEM((early * block, tile_cols), jnp.bfloat16),
            pltpu.VMEM((count * span + block, block), jnp.bfloat16),
            pltpu.VMEM((count, block), jnp.int32),
            pltpu.SMEM((count, block), jnp.int32),
            pltpu.SMEM((row_blocks + 1,), jnp.int32),
            pltpu.SMEM((row_blocks + 1, early), jnp.int32),
            pltpu.SMEM((row_blocks + 1, early), jnp.int32),
            pltpu.SemaphoreType.DMA((3,)),
        ],
        compiler_params=pltpu.CompilerParams(vmem_limit_bytes=early_bytes + passed_bytes + SLACK),
        name="early_product",
    )(
        jnp.stack([my_row, my_col]).astype(jnp.int32),
        jnp.array(offsets, jnp.int32),
        *record_arrays,
        *[p[0] for p in pieces],
    )
    return pl.pallas_call(
        functools.partial(late_kernel, dims),
        out_shape=jax.ShapeDtypeStruct((tile_rows, tile_cols), term_previous.dtype),
        in_specs=[smem, vmem, vmem, vmem] + [vmem] * len(final),
        out_specs=anywhere,
        scratch_shapes=[
            pltpu.VMEM((tile_rows, tile_cols), term_previous.dtype),
            pltpu.SemaphoreType.DMA,
        ],
        compiler_params=pltpu.CompilerParams(vmem_limit_bytes=passed_bytes + 4 * tile_rows * tile_cols + SLACK),
        name="late_product",
    )(keep_mask, acc, late, term_previous, *final)


def solution(mesh):
    placed = (
        P("row", "col", None, None),
        P("row", "col"),
        P("row", "col"),
        P(None, "row", "col"),
        P("row", "col"),
        P("row", "col"),
    )
    return jax.shard_map(
        per_device, mesh=mesh, in_specs=placed, out_specs=P("row", "col"), check_vma=False
    )
```

```python
import functools

import jax
import jax.numpy as jnp
from jax import lax
from jax.experimental import pallas as pl
from jax.experimental.pallas import tpu as pltpu
from jax.sharding import PartitionSpec as P

SMALL = 1024 * 1024
SLACK = 5 * 1024 * 1024
PAD = 16
TILE = 256


def swap(x, axis, offset):
    size = lax.axis_size(axis)
    return lax.ppermute(x, axis, [(i, i ^ offset) for i in range(size)])


def join_kernel(*refs):
    parts, out, sems = refs[:-2], refs[-2], refs[-1]
    copies, at = [], 0
    for n, part in enumerate(parts):
        rows = pl.ds(at, part.shape[0])
        copies.append(pltpu.make_async_copy(part, out.at[rows], sems.at[n]))
        copies[-1].start()
        at += part.shape[0]
    for copy in copies:
        copy.wait()


def join(parts):
    rows = sum(part.shape[0] for part in parts)
    return pl.pallas_call(
        join_kernel,
        out_shape=jax.ShapeDtypeStruct((rows, parts[0].shape[1]), parts[0].dtype),
        in_specs=[pl.BlockSpec(memory_space=pl.ANY)] * len(parts),
        out_specs=pl.BlockSpec(memory_space=pl.ANY),
        scratch_shapes=[pltpu.SemaphoreType.DMA((len(parts),))],
        compiler_params=pltpu.CompilerParams(vmem_limit_bytes=SMALL),
        name="join",
    )(*parts)


def hold_kernel(*refs):
    pass


def hold(array, others):
    return pl.pallas_call(
        hold_kernel,
        out_shape=jax.ShapeDtypeStruct(array.shape, array.dtype),
        in_specs=[pl.BlockSpec(memory_space=pl.ANY)] * (1 + len(others)),
        out_specs=pl.BlockSpec(memory_space=pl.ANY),
        input_output_aliases={0: 0},
        compiler_params=pltpu.CompilerParams(vmem_limit_bytes=SMALL),
        name="hold",
    )(array, *others)


def split(number, size):
    if size & (size - 1) == 0:
        return number >> (size.bit_length() - 1), number & (size - 1)
    return number // size, number % size


def early_kernel(dims, arrays, early, routes, spot, offsets, *refs):
    grid_rows, grid_cols, slots, panels, block = dims
    span = slots * block + PAD
    per_row = grid_cols // grid_rows
    record_refs = refs[:arrays]
    term_refs = refs[arrays:-10]
    acc, late, terms, held, code_rows, codes, counts, firsts, depths, sems = refs[-10:]
    row_blocks = acc.shape[0] // block
    count = grid_rows * grid_cols
    nothing = count * span

    def fetch(copies):
        for copy in copies:
            copy.start()
        return copies

    at, first = 0, []
    for ref in record_refs:
        rows = pl.ds(at, ref.shape[0])
        first.append(pltpu.make_async_copy(ref, held.at[rows], sems.at[0]))
        at += ref.shape[0]
    first = fetch(first)
    second = []
    for ref, route in zip(term_refs, routes):
        for source, target, size in route:
            here, there = pl.ds(source, size), pl.ds(target, size)
            second.append(pltpu.make_async_copy(ref.at[here], terms.at[there], sems.at[1]))
    second = fetch(second)
    late[...] = jnp.zeros_like(late)
    held[pl.ds(nothing, block), :] = jnp.zeros((block, held.shape[1]), held.dtype)

    def clear(i, carry):
        counts[i] = 0
        for n in range(early):
            firsts[i, n] = nothing
            depths[i, n] = 0
        return carry

    lax.fori_loop(0, row_blocks + 1, clear, 0, unroll=True)
    for copy in first:
        copy.wait()
    for n in range(count):
        row = held[pl.ds(n * span + slots * block, PAD), :].astype(jnp.float32)
        code_rows[pl.ds(n, 1), :] = row[:1].astype(jnp.int32)
    to_scalars = pltpu.make_async_copy(code_rows, codes, sems.at[2])
    to_scalars.start()
    to_scalars.wait()
    my_row, my_col = spot[0], spot[1]

    def place(n, carry):
        source, inner = split(my_col ^ offsets[split(n, grid_rows)[0]], per_row)
        source = source ^ my_row
        for j in range(slots):
            code = codes[n, j]
            row, panel = split(code, panels)
            k = (source * panels + panel) * per_row + inner
            record = pl.multiple_of(n * span + j * block, PAD)

            to = jnp.where((code >= 0) & (k < early), row, row_blocks)
            at = counts[to]
            firsts[to, jnp.minimum(at, early - 1)] = record
            depths[to, jnp.minimum(at, early - 1)] = k * block
            counts[to] = at + 1

            @pl.when((code >= 0) & (k >= early))
            def _():
                to = pl.ds(pl.multiple_of(row * block, block), block)
                late[k - early, to, :] = 2 * held[pl.ds(record, block), :]

        return carry

    lax.fori_loop(0, count, place, 0, unroll=True)
    for copy in second:
        copy.wait()

    def pair(i, n):
        def one(m):
            left = held[pl.ds(pl.multiple_of(firsts[i, m], PAD), block), :]
            right = terms[pl.ds(pl.multiple_of(depths[i, m], block), block), :]
            return left, right

        (left0, right0), (left1, right1) = one(2 * n), one(2 * n + 1)
        return jnp.dot(
            jnp.concatenate([left0, left1], axis=1),
            jnp.concatenate([right0, right1], axis=0),
            preferred_element_type=jnp.float32,
        )

    for i in range(row_blocks):
        rows = pl.ds(i * block, block)
        product = pair(i, 0) + pair(i, 1)
        acc[rows, :] = 2.0 * product

    def more(i, carry):
        rows = pl.ds(pl.multiple_of(i * block, block), block)

        def step(n, inner):
            acc[rows, :] += 2.0 * pair(i, n)
            return inner

        return lax.fori_loop(2, (counts[i] + 1) >> 1, step, carry)

    lax.fori_loop(0, row_blocks, more, 0)


def late_kernel(dims, keep, acc, late, previous, *refs):
    block = dims[-1]
    term_refs, out, staged, sem = refs[:-3], *refs[-3:]
    blocks = late.shape[0]
    steps = acc.shape[0] // TILE
    right = jnp.concatenate([ref[...] for ref in term_refs], axis=0)
    copies = []
    for t in range(steps):
        rows = pl.ds(t * TILE, TILE)
        left = jnp.concatenate([late[k, rows, :] for k in range(blocks)], axis=1)
        product = jnp.dot(left, right, preferred_element_type=jnp.float32)
        update = acc[rows, :] + product - previous[rows, :].astype(jnp.float32)
        for i in range(TILE // block):
            for j in range(out.shape[1] // block):
                wanted = keep[t * (TILE // block) + i, j] > 0
                part = update[i * block : (i + 1) * block, j * block : (j + 1) * block]
                staged[pl.ds(t * TILE + i * block, block), pl.ds(j * block, block)] = jnp.where(
                    wanted, part, jnp.zeros_like(part)
                ).astype(out.dtype)
        copies.append(pltpu.make_async_copy(staged.at[rows], out.at[rows], sem))
        copies[-1].start()
    for copy in copies:
        copy.wait()


def per_device(send_blocks, send_count, send_place, term_current, term_previous, keep_mask):
    grid_rows, grid_cols = lax.axis_size("row"), lax.axis_size("col")
    my_row, my_col = lax.axis_index("row"), lax.axis_index("col")
    block = send_blocks.shape[-1]
    slots = send_blocks.shape[1]
    panels = term_current.shape[0]
    tile_rows, tile_cols = term_previous.shape
    row_blocks = tile_rows // block
    per_row = grid_cols // grid_rows
    dims = (grid_rows, grid_cols, slots, panels, block)

    lane = jnp.arange(slots, dtype=jnp.int32)
    places = jnp.where(lane[None, :] < send_count, send_place, -1).astype(jnp.bfloat16)
    pad = jnp.broadcast_to(
        jnp.pad(places, ((0, 0), (0, block - slots)))[:, None, :], (grid_rows, PAD, block)
    )

    def payload(offset):
        to = my_row ^ offset
        records = lax.dynamic_index_in_dim(send_blocks, to, 0, keepdims=False)
        tail = lax.dynamic_index_in_dim(pad, to, 0, keepdims=False)
        return jnp.concatenate([records.reshape(slots * block, block), tail], axis=0)

    got = [swap(payload(o), "row", o) for o in range(1, grid_rows)]

    last = grid_rows - 1
    rows = term_current.shape[1]
    flat = term_current.reshape(panels * rows, tile_cols)
    pieces = [(flat, [(0, 0, panels * rows)])]
    if grid_rows == 4 and panels == 2:
        size = panels * rows
        flat = hold(flat, got)
        up, down = swap(flat, "row", 1), swap(flat, "row", 2)
        pieces += [(up, [(0, size, size)]), (down, [(0, 2 * size, size)])]
        at = rows + PAD
        final = [swap(up[:at], "row", 2), swap(down[at:], "row", 1)]
    else:
        for o in range(1, last):
            pieces.append((swap(flat, "row", o), [(0, o * panels * rows, panels * rows)]))
        final = [swap(flat[p * rows : (p + 1) * rows], "row", last) for p in range(panels)]

    own = join([payload(0)] + got)
    if grid_cols == 8:
        far, near = swap(own, "col", 6), swap(own, "col", 2)
        middle = swap(far, "col", 2)
        offsets = [0, 6, 2, 4]
        groups = [jnp.concatenate([own, far], axis=0), near, middle]
        parts = groups
        others = [swap(group, "col", 1) for group in groups]
    else:
        offsets = list(range(0, grid_cols, 2))
        parts = [own] + [swap(own, "col", o) for o in offsets[1:]]
        others = [swap(part, "col", 1) for part in parts]
    offsets = offsets + [o ^ 1 for o in offsets]
    record_arrays = parts + others
    span = slots * block + PAD

    early = (grid_rows - 1) * panels * per_row
    anywhere = pl.BlockSpec(memory_space=pl.ANY)
    smem = pl.BlockSpec(memory_space=pltpu.SMEM)
    vmem = pl.BlockSpec(memory_space=pltpu.VMEM)
    late_blocks = panels * per_row
    count = grid_cols * grid_rows
    early_bytes = 2 * (early * block * tile_cols + count * span * block)
    passed_bytes = 4 * tile_rows * tile_cols + 2 * late_blocks * tile_rows * block
    acc, late = pl.pallas_call(
        functools.partial(early_kernel, dims, len(record_arrays), early, [p[1] for p in pieces]),
        out_shape=[
            jax.ShapeDtypeStruct((tile_rows, tile_cols), jnp.float32),
            jax.ShapeDtypeStruct((late_blocks, tile_rows, block), jnp.bfloat16),
        ],
        in_specs=[smem, smem] + [anywhere] * (len(record_arrays) + len(pieces)),
        out_specs=[vmem, vmem],
        scratch_shapes=[
            pltpu.VMEM((early * block, tile_cols), jnp.bfloat16),
            pltpu.VMEM((count * span + block, block), jnp.bfloat16),
            pltpu.VMEM((count, block), jnp.int32),
            pltpu.SMEM((count, block), jnp.int32),
            pltpu.SMEM((row_blocks + 1,), jnp.int32),
            pltpu.SMEM((row_blocks + 1, early), jnp.int32),
            pltpu.SMEM((row_blocks + 1, early), jnp.int32),
            pltpu.SemaphoreType.DMA((3,)),
        ],
        compiler_params=pltpu.CompilerParams(vmem_limit_bytes=early_bytes + passed_bytes + SLACK),
        name="early_product",
    )(
        jnp.stack([my_row, my_col]).astype(jnp.int32),
        jnp.array(offsets, jnp.int32),
        *record_arrays,
        *[p[0] for p in pieces],
    )
    return pl.pallas_call(
        functools.partial(late_kernel, dims),
        out_shape=jax.ShapeDtypeStruct((tile_rows, tile_cols), term_previous.dtype),
        in_specs=[smem, vmem, vmem, vmem] + [vmem] * len(final),
        out_specs=anywhere,
        scratch_shapes=[
            pltpu.VMEM((tile_rows, tile_cols), term_previous.dtype),
            pltpu.SemaphoreType.DMA,
        ],
        compiler_params=pltpu.CompilerParams(vmem_limit_bytes=passed_bytes + 4 * tile_rows * tile_cols + SLACK),
        name="late_product",
    )(keep_mask, acc, late, term_previous, *final)


def solution(mesh):
    placed = (
        P("row", "col", None, None),
        P("row", "col"),
        P("row", "col"),
        P(None, "row", "col"),
        P("row", "col"),
        P("row", "col"),
    )
    return jax.shard_map(
        per_device, mesh=mesh, in_specs=placed, out_specs=P("row", "col"), check_vma=False
    )
```

```python
import functools

import jax
import jax.numpy as jnp
from jax import lax
from jax.experimental import pallas as pl
from jax.experimental.pallas import tpu as pltpu
from jax.sharding import PartitionSpec as P

SMALL = 1024 * 1024
SLACK = 5 * 1024 * 1024
PAD = 16
TILE = 256


def swap(x, axis, offset):
    size = lax.axis_size(axis)
    return lax.ppermute(x, axis, [(i, i ^ offset) for i in range(size)])


def join_kernel(*refs):
    parts, out, sems = refs[:-2], refs[-2], refs[-1]
    copies, at = [], 0
    for n, part in enumerate(parts):
        rows = pl.ds(at, part.shape[0])
        copies.append(pltpu.make_async_copy(part, out.at[rows], sems.at[n]))
        copies[-1].start()
        at += part.shape[0]
    for copy in copies:
        copy.wait()


def join(parts):
    rows = sum(part.shape[0] for part in parts)
    return pl.pallas_call(
        join_kernel,
        out_shape=jax.ShapeDtypeStruct((rows, parts[0].shape[1]), parts[0].dtype),
        in_specs=[pl.BlockSpec(memory_space=pl.ANY)] * len(parts),
        out_specs=pl.BlockSpec(memory_space=pl.ANY),
        scratch_shapes=[pltpu.SemaphoreType.DMA((len(parts),))],
        compiler_params=pltpu.CompilerParams(vmem_limit_bytes=SMALL),
        name="join",
    )(*parts)


def hold_kernel(*refs):
    pass


def hold(array, others):
    return pl.pallas_call(
        hold_kernel,
        out_shape=jax.ShapeDtypeStruct(array.shape, array.dtype),
        in_specs=[pl.BlockSpec(memory_space=pl.ANY)] * (1 + len(others)),
        out_specs=pl.BlockSpec(memory_space=pl.ANY),
        input_output_aliases={0: 0},
        compiler_params=pltpu.CompilerParams(vmem_limit_bytes=SMALL),
        name="hold",
    )(array, *others)


def split(number, size):
    if size & (size - 1) == 0:
        return number >> (size.bit_length() - 1), number & (size - 1)
    return number // size, number % size


def early_kernel(dims, arrays, early, routes, spot, offsets, *refs):
    grid_rows, grid_cols, slots, panels, block = dims
    span = slots * block + PAD
    per_row = grid_cols // grid_rows
    record_refs = refs[:arrays]
    term_refs = refs[arrays:-10]
    acc, late, terms, held, code_rows, codes, counts, firsts, depths, sems = refs[-10:]
    row_blocks = acc.shape[0] // block
    count = grid_rows * grid_cols
    nothing = count * span

    def fetch(copies):
        for copy in copies:
            copy.start()
        return copies

    at, first = 0, []
    for ref in record_refs:
        rows = pl.ds(at, ref.shape[0])
        first.append(pltpu.make_async_copy(ref, held.at[rows], sems.at[0]))
        at += ref.shape[0]
    first = fetch(first)
    second = []
    for ref, route in zip(term_refs, routes):
        for source, target, size in route:
            here, there = pl.ds(source, size), pl.ds(target, size)
            second.append(pltpu.make_async_copy(ref.at[here], terms.at[there], sems.at[1]))
    second = fetch(second)
    late[...] = jnp.zeros_like(late)
    held[pl.ds(nothing, block), :] = jnp.zeros((block, held.shape[1]), held.dtype)

    def clear(i, carry):
        counts[i] = 0
        for n in range(early):
            firsts[i, n] = nothing
            depths[i, n] = 0
        return carry

    lax.fori_loop(0, row_blocks + 1, clear, 0, unroll=True)
    for copy in first:
        copy.wait()
    for n in range(count):
        row = held[pl.ds(n * span + slots * block, PAD), :].astype(jnp.float32)
        code_rows[pl.ds(n, 1), :] = row[:1].astype(jnp.int32)
    to_scalars = pltpu.make_async_copy(code_rows, codes, sems.at[2])
    to_scalars.start()
    to_scalars.wait()
    my_row, my_col = spot[0], spot[1]

    def place(n, carry):
        source, inner = split(my_col ^ offsets[split(n, grid_rows)[0]], per_row)
        source = source ^ my_row
        for j in range(slots):
            code = codes[n, j]
            row, panel = split(code, panels)
            k = (source * panels + panel) * per_row + inner
            record = pl.multiple_of(n * span + j * block, PAD)

            to = jnp.where((code >= 0) & (k < early), row, row_blocks)
            at = counts[to]
            firsts[to, jnp.minimum(at, early - 1)] = record
            depths[to, jnp.minimum(at, early - 1)] = k * block
            counts[to] = at + 1

            @pl.when((code >= 0) & (k >= early))
            def _():
                to = pl.ds(pl.multiple_of(row * block, block), block)
                late[k - early, to, :] = 2 * held[pl.ds(record, block), :]

        return carry

    lax.fori_loop(0, count, place, 0, unroll=True)
    for copy in second:
        copy.wait()

    def pair(i, n):
        def one(m):
            left = held[pl.ds(pl.multiple_of(firsts[i, m], PAD), block), :]
            right = terms[pl.ds(pl.multiple_of(depths[i, m], block), block), :]
            return left, right

        (left0, right0), (left1, right1) = one(2 * n), one(2 * n + 1)
        return jnp.dot(
            jnp.concatenate([left0, left1], axis=1),
            jnp.concatenate([right0, right1], axis=0),
            preferred_element_type=jnp.float32,
        )

    for i in range(row_blocks):
        rows = pl.ds(i * block, block)
        product = pair(i, 0) + pair(i, 1)
        acc[rows, :] = 2.0 * product

    def more(i, carry):
        rows = pl.ds(pl.multiple_of(i * block, block), block)

        def step(n, inner):
            acc[rows, :] += 2.0 * pair(i, n)
            return inner

        return lax.fori_loop(2, (counts[i] + 1) >> 1, step, carry)

    lax.fori_loop(0, row_blocks, more, 0)


def late_kernel(dims, keep, acc, late, previous, *refs):
    block = dims[-1]
    term_refs, out, staged, sem = refs[:-3], *refs[-3:]
    blocks = late.shape[0]
    whole = acc.shape[0] // TILE - 1
    tiles = [(t * TILE, TILE) for t in range(whole)]
    tiles += [(whole * TILE + i * block, block) for i in range(TILE // block)]
    right = jnp.concatenate([ref[...] for ref in term_refs], axis=0)
    copies = []
    for start, size in tiles:
        rows = pl.ds(start, size)
        left = jnp.concatenate([late[k, rows, :] for k in range(blocks)], axis=1)
        product = jnp.dot(left, right, preferred_element_type=jnp.float32)
        update = acc[rows, :] + product - previous[rows, :].astype(jnp.float32)
        for i in range(size // block):
            for j in range(out.shape[1] // block):
                wanted = keep[start // block + i, j] > 0
                part = update[i * block : (i + 1) * block, j * block : (j + 1) * block]
                staged[pl.ds(start + i * block, block), pl.ds(j * block, block)] = jnp.where(
                    wanted, part, jnp.zeros_like(part)
                ).astype(out.dtype)
        copies.append(pltpu.make_async_copy(staged.at[rows], out.at[rows], sem))
        copies[-1].start()
    for copy in copies:
        copy.wait()


def per_device(send_blocks, send_count, send_place, term_current, term_previous, keep_mask):
    grid_rows, grid_cols = lax.axis_size("row"), lax.axis_size("col")
    my_row, my_col = lax.axis_index("row"), lax.axis_index("col")
    block = send_blocks.shape[-1]
    slots = send_blocks.shape[1]
    panels = term_current.shape[0]
    tile_rows, tile_cols = term_previous.shape
    row_blocks = tile_rows // block
    per_row = grid_cols // grid_rows
    dims = (grid_rows, grid_cols, slots, panels, block)

    lane = jnp.arange(slots, dtype=jnp.int32)
    places = jnp.where(lane[None, :] < send_count, send_place, -1).astype(jnp.bfloat16)
    pad = jnp.broadcast_to(
        jnp.pad(places, ((0, 0), (0, block - slots)))[:, None, :], (grid_rows, PAD, block)
    )

    def payload(offset):
        to = my_row ^ offset
        records = lax.dynamic_index_in_dim(send_blocks, to, 0, keepdims=False)
        tail = lax.dynamic_index_in_dim(pad, to, 0, keepdims=False)
        return jnp.concatenate([records.reshape(slots * block, block), tail], axis=0)

    got = [swap(payload(o), "row", o) for o in range(1, grid_rows)]

    last = grid_rows - 1
    rows = term_current.shape[1]
    flat = term_current.reshape(panels * rows, tile_cols)
    pieces = [(flat, [(0, 0, panels * rows)])]
    if grid_rows == 4 and panels == 2:
        size = panels * rows
        flat = hold(flat, got)
        up, down = swap(flat, "row", 1), swap(flat, "row", 2)
        pieces += [(up, [(0, size, size)]), (down, [(0, 2 * size, size)])]
        at = rows + PAD
        final = [swap(up[:at], "row", 2), swap(down[at:], "row", 1)]
    else:
        for o in range(1, last):
            pieces.append((swap(flat, "row", o), [(0, o * panels * rows, panels * rows)]))
        final = [swap(flat[p * rows : (p + 1) * rows], "row", last) for p in range(panels)]

    own = join([payload(0)] + got)
    if grid_cols == 8:
        far, near = swap(own, "col", 6), swap(own, "col", 2)
        middle = swap(far, "col", 2)
        offsets = [0, 6, 2, 4]
        groups = [jnp.concatenate([own, far], axis=0), near, middle]
        parts = groups
        others = [swap(group, "col", 1) for group in groups]
    else:
        offsets = list(range(0, grid_cols, 2))
        parts = [own] + [swap(own, "col", o) for o in offsets[1:]]
        others = [swap(part, "col", 1) for part in parts]
    offsets = offsets + [o ^ 1 for o in offsets]
    record_arrays = parts + others
    span = slots * block + PAD

    early = (grid_rows - 1) * panels * per_row
    anywhere = pl.BlockSpec(memory_space=pl.ANY)
    smem = pl.BlockSpec(memory_space=pltpu.SMEM)
    vmem = pl.BlockSpec(memory_space=pltpu.VMEM)
    late_blocks = panels * per_row
    count = grid_cols * grid_rows
    early_bytes = 2 * (early * block * tile_cols + count * span * block)
    passed_bytes = 4 * tile_rows * tile_cols + 2 * late_blocks * tile_rows * block
    acc, late = pl.pallas_call(
        functools.partial(early_kernel, dims, len(record_arrays), early, [p[1] for p in pieces]),
        out_shape=[
            jax.ShapeDtypeStruct((tile_rows, tile_cols), jnp.float32),
            jax.ShapeDtypeStruct((late_blocks, tile_rows, block), jnp.bfloat16),
        ],
        in_specs=[smem, smem] + [anywhere] * (len(record_arrays) + len(pieces)),
        out_specs=[vmem, vmem],
        scratch_shapes=[
            pltpu.VMEM((early * block, tile_cols), jnp.bfloat16),
            pltpu.VMEM((count * span + block, block), jnp.bfloat16),
            pltpu.VMEM((count, block), jnp.int32),
            pltpu.SMEM((count, block), jnp.int32),
            pltpu.SMEM((row_blocks + 1,), jnp.int32),
            pltpu.SMEM((row_blocks + 1, early), jnp.int32),
            pltpu.SMEM((row_blocks + 1, early), jnp.int32),
            pltpu.SemaphoreType.DMA((3,)),
        ],
        compiler_params=pltpu.CompilerParams(vmem_limit_bytes=early_bytes + passed_bytes + SLACK),
        name="early_product",
    )(
        jnp.stack([my_row, my_col]).astype(jnp.int32),
        jnp.array(offsets, jnp.int32),
        *record_arrays,
        *[p[0] for p in pieces],
    )
    return pl.pallas_call(
        functools.partial(late_kernel, dims),
        out_shape=jax.ShapeDtypeStruct((tile_rows, tile_cols), term_previous.dtype),
        in_specs=[smem, vmem, vmem, vmem] + [vmem] * len(final),
        out_specs=anywhere,
        scratch_shapes=[
            pltpu.VMEM((tile_rows, tile_cols), term_previous.dtype),
            pltpu.SemaphoreType.DMA,
        ],
        compiler_params=pltpu.CompilerParams(vmem_limit_bytes=passed_bytes + 4 * tile_rows * tile_cols + SLACK),
        name="late_product",
    )(keep_mask, acc, late, term_previous, *final)


def solution(mesh):
    placed = (
        P("row", "col", None, None),
        P("row", "col"),
        P("row", "col"),
        P(None, "row", "col"),
        P("row", "col"),
        P("row", "col"),
    )
    return jax.shard_map(
        per_device, mesh=mesh, in_specs=placed, out_specs=P("row", "col"), check_vma=False
    )
```
